32 devices in a mesh: coh: 4 (over z), lat: 4 (over x, core), lon: 2 (over y).
Axes of the slice: x: 2, y: 2, z: 4, core: 2. Of those that a mesh axis runs over, the one named last changes fastest.
Arguments:
- saved_period_abundance: bfloat16 [2, 128, 256, 512], P(None, 'coh', 'lat', 'lon'), may hold values from 0.099609375 to 2
- final_abundance_sensitivity: bfloat16 [128, 256, 512], P('coh', 'lat', 'lon'), may hold values from -6 to 6
- prey_biomass: float32 [2, 256, 512], P(None, 'lat', 'lon'), may hold values from 0.2 to 2
- water_heat_field: float32 [2, 256, 512], P(None, 'lat', 'lon'), may hold values from 10 to 30
- marine_indicator: int32 [256, 512], P('lat', 'lon'), may hold values 0 or 1
- fishing_pressure: float32 [256, 512], P('lat', 'lon'), may hold values from 0.1 to 2
- offspring_yield: float32 [256, 512], P('lat', 'lon'), may hold values from 2 to 20
- death_fraction: float32 [128], P('coh'), may hold values from 0.01 to 0.5
- gear_vulnerability: float32 [128], P('coh'), may hold values from 0.05 to 0.5
- spreading_coefficient: float32 [128], P('coh'), may hold values from 0.02 to 0.12
- directed_drift_rate: float32 [128], P('coh'), may hold values from 0.01 to 0.06
- favoured_thermal_level: float32 [128], P('coh'), may hold values from 12 to 28
- breeding_contribution: float32 [128], P('coh'), may hold values from 0.005 to 0.03
- landing_error_sensitivity: float32 [256, 2, 128], P(('lat', 'lon'), None, 'coh'), may hold values from -6 to 6
- fleet_east_piece: int32 [256, 1], P(('lat', 'lon')), may hold values from 0 to 1; in each aligned block of 32 rows (0 to 31, 32 to 63, ...) at most 16 rows name the same one
- fleet_north_piece: int32 [256], P(('lat', 'lon')), may hold values from 0 to 3
- fleet_area_patch: int32 [256], P(('lat', 'lon')), may hold values from 0 to 31
- fleet_age_bounds: int32 [256, 2], P(('lat', 'lon')), may hold values from 0 to 128, as said below
Outputs:
- density_grad: float32 [128, 256, 512], P('coh', 'lat', 'lon')
- recruit_grad: float32 [256, 512], P('lat', 'lon')
The draws below stay inside these ranges and needn't reach their ends.
Inputs may be any that keep to these rules, and one draw needn't show every extreme that they name: `fleet_east_piece`: among the rows of one device, at most 16 name the same longitude tile, and some longitude tile is named by exactly 16 of them. `fleet_age_bounds`: in every row the first entry is below the second.
All inputs are finite; a program needn't handle non-finite values. No bound on the sum of `marine_indicator` on one device may be relied on, other than what follows from the above.
Results may differ from the reference program's by a relative error of at most 0.0003.
Values sent between devices are 32-bit elements; how exact they have to be, the bound alone decides.
No kernel may reach another device: no remote copies, remote signals or barrier semaphores. Data moves between devices by JAX's collectives and lax.ppermute only.
A program may use at most 64 MiB of HBM per device.

```python
import math
import jax
import jax.numpy as jnp
import numpy as np
from jax import lax

AGE_CLASSES = 128
CY = 64
CX = 256
TIME_PERIODS = 2
BY = 16
BX = 32
ROWS_DEV = 32
FLEET = 256
CAP = 16
BLOCKS = 32
NORTH_SOUTH_LINES = 256
EAST_WEST_LINES = 512
N_LAT = 4
N_LON = 2


def draw_fleet_age_bounds(key, part):
    picks = jax.random.randint(jax.random.fold_in(key, 7), (FLEET, 2), 0, AGE_CLASSES)
    lower = jnp.minimum(picks[:, 0], picks[:, 1])
    upper = jnp.maximum(picks[:, 0], picks[:, 1]) + 1
    return jnp.stack([lower, upper], axis=1).astype(jnp.int32)


def set_ends(drawn, stream_key, low, high):
    shape = drawn.shape
    spot = [jax.random.randint(jax.random.fold_in(stream_key, axis), (), 0, shape[axis]) for axis in range(len(shape))]
    drawn = drawn.at[tuple(spot)].set(low)
    longest = shape.index(max(shape))
    spot[longest] = (spot[longest] + 1) % shape[longest]
    return drawn.at[tuple(spot)].set(high)


def block_levels(rng, shape, pieces, smallest, largest):
    gain, own = 1.0, jax.random.fold_in(rng, 6)
    for axis_at, parts in pieces:
        draws = jnp.exp(jax.random.uniform(jax.random.fold_in(own, axis_at), (parts,), jnp.float32, smallest / len(pieces), largest / len(pieces)))
        gain = gain * jnp.repeat(draws, shape[axis_at] // parts).reshape([-1 if axis == axis_at else 1 for axis in range(len(shape))])
    return gain


def deal_out(own_key, own, number, rows, number_of, top, most, lean):
    order = jax.random.permutation(own_key, number_of)
    heavy_load, common = portions_of(number_of, rows * top, most, lean, True), portions_of(number_of, rows * top, most, lean, False)
    places = jnp.arange(number_of)

    def named(tallies, rotation):
        used = int((tallies > 0).sum())
        fixed = max(1, used // 4)
        passed = fixed + (places - fixed + rotation * (used - fixed)) % max(1, number_of - fixed)
        return jnp.zeros((number_of,), jnp.int32).at[order[jnp.where(places < fixed, places, passed)]].set(jnp.asarray(tallies, jnp.int32))

    tallies = jnp.where(number % 4 == 0, named(heavy_load, number // 4), named(common, number - number // 4 - 1))
    mixed = jax.random.permutation(jax.random.fold_in(own, 3), number_of)
    giver, receiver = mixed[0:number_of // 2 * 2:2], mixed[1:number_of // 2 * 2:2]
    slack = jnp.minimum(tallies[giver] - 1, most - tallies[receiver]) // 2
    slack = jnp.where((giver == order[0]) | (receiver == order[0]) | (tallies[receiver] == 0), 0, jnp.maximum(slack, 0))
    passed = jax.random.randint(jax.random.fold_in(own, 4), (number_of // 2,), 0, 1 << 20) % (slack + 1)
    tallies = tallies.at[giver].add(-passed).at[receiver].add(passed)
    labels = jnp.searchsorted(jnp.cumsum(tallies), jnp.arange(rows * top), side="right").astype(jnp.int32)
    listing = labels.reshape(top, rows).T
    listing = listing[jax.random.permutation(jax.random.fold_in(own, 1), rows)]
    rotation = jax.random.randint(jax.random.fold_in(own, 2), (rows, 1), 0, top)
    return jnp.take_along_axis(listing, (jnp.arange(top)[None, :] + rotation) % top, axis=1)


def portions_of(amount, total, bound, lean, full):
    weights = [(1 << 20) // math.isqrt(grade ** lean) + 1 for grade in range(1, amount + 1)]
    largest = bound if full else min(bound, max(-(-total // amount), total * weights[0] // sum(weights)))
    least = 1 if total - largest >= amount - 1 else 0
    given, surplus = [largest] + [least] * (amount - 1), total - largest - least * (amount - 1)
    while surplus > 0:
        candidates = [i for i in range(1, amount) if given[i] < largest] or [i for i in range(1, amount) if given[i] < bound]
        whole, remaining = sum([weights[i] for i in candidates]), surplus
        for i in candidates:
            more = min(bound - given[i], max(1, remaining * weights[i] // whole), surplus)
            given[i] = given[i] + more
            surplus = surplus - more
    return np.array(given)


def gaussian(own_key, extent, width, reach, cuts=(), dtype=jnp.bfloat16):
    result = width * jax.random.normal(own_key, extent, jnp.float32)
    if cuts:
        result = result * block_levels(own_key, extent, cuts, -0.22, 0.18)
    return jnp.clip(result, -reach, reach).astype(dtype)


def setup_inputs(seed: int = 0) -> dict:
    splits = jax.random.split(jax.random.key(seed), 19)
    saved_period_abundance = jnp.clip(jnp.exp(math.log(2.0) - 2.9996462 * jax.random.uniform(splits[0], (TIME_PERIODS, AGE_CLASSES, NORTH_SOUTH_LINES, EAST_WEST_LINES), jnp.float32) ** block_levels(splits[0], (TIME_PERIODS, AGE_CLASSES, NORTH_SOUTH_LINES, EAST_WEST_LINES), ((1, 4), (2, 4), (3, 2)), -0.2, 0.2)), 0.099609375, 2.0).astype(jnp.bfloat16)
    final_abundance_sensitivity = gaussian(splits[1], (AGE_CLASSES, NORTH_SOUTH_LINES, EAST_WEST_LINES), 1.0, 6.0, ((0, 4), (1, 4), (2, 2)))
    prey_biomass = jnp.clip(jnp.exp(math.log(2.0) - 2.3025851 * jax.random.uniform(splits[2], (TIME_PERIODS, NORTH_SOUTH_LINES, EAST_WEST_LINES), jnp.float32) ** block_levels(splits[2], (TIME_PERIODS, NORTH_SOUTH_LINES, EAST_WEST_LINES), ((1, 4), (2, 2)), -0.2, 0.2)), 0.2, 2.0)
    water_heat_field = jnp.clip(10.0 + 20.0 * jax.random.uniform(splits[3], (TIME_PERIODS, NORTH_SOUTH_LINES, EAST_WEST_LINES), jnp.float32) ** block_levels(splits[3], (TIME_PERIODS, NORTH_SOUTH_LINES, EAST_WEST_LINES), ((1, 4), (2, 2)), -0.2, 0.2), 10.0, 30.0)
    marine_indicator = set_ends((jax.random.randint(splits[4], (NORTH_SOUTH_LINES, EAST_WEST_LINES), 0, 5) < 4).astype(jnp.int32), jax.random.fold_in(splits[4], 1), 0, 1)
    fishing_pressure = jnp.clip(jnp.exp(math.log(2.0) - 2.9957323 * jax.random.uniform(splits[5], (NORTH_SOUTH_LINES, EAST_WEST_LINES), jnp.float32) ** block_levels(splits[5], (NORTH_SOUTH_LINES, EAST_WEST_LINES), ((0, 4), (1, 2)), -0.2, 0.2)), 0.1, 2.0)
    offspring_yield = jnp.clip(jnp.exp(math.log(20.0) - 2.3025851 * jax.random.uniform(splits[6], (NORTH_SOUTH_LINES, EAST_WEST_LINES), jnp.float32) ** block_levels(splits[6], (NORTH_SOUTH_LINES, EAST_WEST_LINES), ((0, 4), (1, 2)), -0.2, 0.2)), 2.0, 20.0)
    death_fraction = jnp.clip(jnp.exp(math.log(0.5) - 3.912023 * jax.random.uniform(splits[7], (AGE_CLASSES,), jnp.float32) ** block_levels(splits[7], (AGE_CLASSES,), ((0, 4),), -0.2, 0.2)), 0.01, 0.5)
    gear_vulnerability = jnp.clip(jnp.exp(math.log(0.5) - 2.3025851 * jax.random.uniform(splits[8], (AGE_CLASSES,), jnp.float32) ** block_levels(splits[8], (AGE_CLASSES,), ((0, 4),), -0.2, 0.2)), 0.05, 0.5)
    spreading_coefficient = jnp.clip(jnp.exp(math.log(0.12) - 1.7917595 * jax.random.uniform(splits[9], (AGE_CLASSES,), jnp.float32) ** block_levels(splits[9], (AGE_CLASSES,), ((0, 4),), -0.2, 0.2)), 0.02, 0.12)
    directed_drift_rate = jnp.clip(jnp.exp(math.log(0.06) - 1.7917595 * jax.random.uniform(splits[10], (AGE_CLASSES,), jnp.float32) ** block_levels(splits[10], (AGE_CLASSES,), ((0, 4),), -0.2, 0.2)), 0.01, 0.06)
    favoured_thermal_level = jnp.clip(12.0 + 16.0 * jax.random.uniform(splits[11], (AGE_CLASSES,), jnp.float32) ** block_levels(splits[11], (AGE_CLASSES,), ((0, 4),), -0.2, 0.2), 12.0, 28.0)
    breeding_contribution = jnp.clip(jnp.exp(math.log(0.03) - 1.7917595 * jax.random.uniform(splits[12], (AGE_CLASSES,), jnp.float32) ** block_levels(splits[12], (AGE_CLASSES,), ((0, 4),), -0.2, 0.2)), 0.005, 0.03)
    landing_error_sensitivity = gaussian(splits[13], (FLEET, TIME_PERIODS, AGE_CLASSES), 1.0, 6.0, ((0, 8), (2, 4)), jnp.float32)
    fleet_east_piece_keys = jax.random.split(jax.random.fold_in(splits[14], 1), FLEET // ROWS_DEV)
    fleet_east_piece_turns = jax.random.permutation(jax.random.fold_in(splits[14], 3), FLEET // ROWS_DEV)
    fleet_east_piece = jax.vmap(lambda own, number: deal_out(jax.random.fold_in(splits[14], 2), own, number, ROWS_DEV, N_LON, 1, CAP, 2))(fleet_east_piece_keys, fleet_east_piece_turns).reshape((FLEET, 1))
    fleet_north_piece = set_ends(jax.random.randint(splits[15], (FLEET,), 0, N_LAT), jax.random.fold_in(splits[15], 1), 0, N_LAT - 1).astype(jnp.int32)
    fleet_area_patch = set_ends(jax.random.randint(splits[16], (FLEET,), 0, BLOCKS), jax.random.fold_in(splits[16], 1), 0, BLOCKS - 1).astype(jnp.int32)
    fleet_age_bounds = draw_fleet_age_bounds(jax.random.fold_in(splits[18], 71), 0)
    return {"saved_period_abundance": saved_period_abundance, "final_abundance_sensitivity": final_abundance_sensitivity, "prey_biomass": prey_biomass, "water_heat_field": water_heat_field, "marine_indicator": marine_indicator, "fishing_pressure": fishing_pressure, "offspring_yield": offspring_yield, "death_fraction": death_fraction, "gear_vulnerability": gear_vulnerability, "spreading_coefficient": spreading_coefficient, "directed_drift_rate": directed_drift_rate, "favoured_thermal_level": favoured_thermal_level, "breeding_contribution": breeding_contribution, "landing_error_sensitivity": landing_error_sensitivity, "fleet_east_piece": fleet_east_piece, "fleet_north_piece": fleet_north_piece, "fleet_area_patch": fleet_area_patch, "fleet_age_bounds": fleet_age_bounds}


thermal_tolerance_spread = 4.0
age_class_bundle = 16
highest = lax.Precision.HIGHEST


def shifted_views(values_in):
    lead = [(0, 0)] * (values_in.ndim - 2)
    padded = jnp.pad(values_in, lead + [(1, 1), (1, 1)])
    return (padded[..., :-2, 1:-1], padded[..., 2:, 1:-1], padded[..., 1:-1, 2:], padded[..., 1:-1, :-2])


def reference(saved_period_abundance, final_abundance_sensitivity, prey_biomass, water_heat_field, marine_indicator, fishing_pressure, offspring_yield, death_fraction, gear_vulnerability, spreading_coefficient, directed_drift_rate, favoured_thermal_level, breeding_contribution, landing_error_sensitivity, fleet_east_piece, fleet_north_piece, fleet_area_patch, fleet_age_bounds):
    sea_field = marine_indicator.astype(jnp.float32)
    cohort_age = jnp.arange(AGE_CLASSES).astype(jnp.int32)
    maturity = (cohort_age + 1).astype(jnp.float32) / AGE_CLASSES * breeding_contribution
    blocks_y = CY // BY
    blocks_x = CX // BX
    grid_y = NORTH_SOUTH_LINES // BY
    grid_x = EAST_WEST_LINES // BX
    block_row = fleet_north_piece * blocks_y + fleet_area_patch // blocks_x
    block_col = fleet_east_piece[:, 0] * blocks_x + fleet_area_patch % blocks_x
    place_id = block_row * grid_x + block_col
    inside = (cohort_age[None, :] >= fleet_age_bounds[:, 0:1]) & (cohort_age[None, :] < fleet_age_bounds[:, 1:2])
    masked = landing_error_sensitivity * inside[:, None, :].astype(jnp.float32)
    onehot = (jnp.arange(grid_y * grid_x).astype(jnp.int32)[:, None] == place_id[None, :]).astype(jnp.float32)
    block_values = jnp.dot(onehot, masked.reshape(FLEET, TIME_PERIODS * AGE_CLASSES), precision=highest)
    block_values = block_values.reshape(grid_y, grid_x, TIME_PERIODS, AGE_CLASSES).transpose(2, 3, 0, 1)
    adjoint = final_abundance_sensitivity.astype(jnp.float32)
    grad_recruit = jnp.zeros((NORTH_SOUTH_LINES, EAST_WEST_LINES), jnp.float32)
    sea_views = shifted_views(sea_field)
    for period_counter in range(TIME_PERIODS - 1, -1, -1):
        density = saved_period_abundance[period_counter].astype(jnp.float32)
        spawning = jnp.tensordot(maturity, density, axes=1, precision=highest)
        first_plane = adjoint[0]
        ratio = 1.0 / (1.0 + spawning)
        recruit_term = first_plane * sea_field * offspring_yield * ratio * ratio
        padded_adj = jnp.concatenate([adjoint, jnp.zeros((1, NORTH_SOUTH_LINES, EAST_WEST_LINES), jnp.float32)], axis=0)
        forage_now = prey_biomass[period_counter]
        present_thermal_field = water_heat_field[period_counter]
        catch_now = block_values[period_counter]

        def group_step(starting_offset):
            later = lax.dynamic_slice_in_dim(padded_adj, starting_offset + 1, age_class_bundle, 0)
            rate_kappa = lax.dynamic_slice_in_dim(spreading_coefficient, starting_offset, age_class_bundle)[:, None, None]
            rate_taxis = lax.dynamic_slice_in_dim(directed_drift_rate, starting_offset, age_class_bundle)[:, None, None]
            mort_part = lax.dynamic_slice_in_dim(death_fraction, starting_offset, age_class_bundle)[:, None, None]
            select_part = lax.dynamic_slice_in_dim(gear_vulnerability, starting_offset, age_class_bundle)[:, None, None]
            ideal_thermal = lax.dynamic_slice_in_dim(favoured_thermal_level, starting_offset, age_class_bundle)[:, None, None]
            mature_part = lax.dynamic_slice_in_dim(maturity, starting_offset, age_class_bundle)[:, None, None]
            thermal_departure = (present_thermal_field[None] - ideal_thermal) / thermal_tolerance_spread
            habitat = sea_field * forage_now / (1.0 + thermal_departure * thermal_departure)
            hab_views = shifted_views(habitat)
            adj_views = shifted_views(later)
            outflow = jnp.zeros_like(later)
            for sea_next, hab_next, adj_next in zip(sea_views, hab_views, adj_views):
                flow_rate = sea_field * sea_next * (rate_kappa + jnp.maximum(rate_taxis * (hab_next - habitat), 0.0))
                outflow = outflow + flow_rate * (later - adj_next)
            after_move = later - outflow
            survive = jnp.exp(-mort_part - select_part * fishing_pressure[None])
            caught = lax.dynamic_slice_in_dim(catch_now, starting_offset, age_class_bundle, 0)
            caught = jnp.repeat(jnp.repeat(caught, BY, axis=1), BX, axis=2)
            return survive * after_move + recruit_term[None] * mature_part + select_part * fishing_pressure[None] * caught

        begins = jnp.arange(AGE_CLASSES // age_class_bundle).astype(jnp.int32) * age_class_bundle
        adjoint = lax.map(group_step, begins).reshape(AGE_CLASSES, NORTH_SOUTH_LINES, EAST_WEST_LINES)
        grad_recruit = grad_recruit + first_plane * sea_field * spawning * ratio
    return adjoint, grad_recruit
```

```python
import functools
import math

import jax
import jax.numpy as jnp
from jax import lax
from jax.experimental import pallas as pl
from jax.experimental.pallas import tpu as pltpu
from jax.sharding import PartitionSpec as P

BY = 16
BX = 32
LANES = 128
SUB = 8
GROUP = 8

f32 = jnp.float32
VMEM = pltpu.MemorySpace.VMEM
SMEM = pltpu.MemorySpace.SMEM
LOG2E = math.log2(math.e)

DEATH, GEAR2, KAPPA, TAU, IDEAL, MAT, GEAR = range(7)


def up_to(value, step):
    return -(-value // step) * step


def whole(memory=VMEM):
    return pl.BlockSpec(memory_space=memory)


def params_of(limit=48):
    return pltpu.CompilerParams(vmem_limit_bytes=limit * 2**20)


def shift(x, axis, distance):
    n = lax.axis_size(axis)
    return lax.ppermute(x, axis, [(i, (i + distance) % n) for i in range(n)])


def swap_edges(ahead, back, both, axis):
    n = lax.axis_size(axis)
    if n == 1:
        return ahead, back
    if n == 2:
        got = shift(both, axis, 1)
        return got, got
    return shift(ahead, axis, 1), shift(back, axis, -1)


def spawn_kernel(months, ages, pos_ref, par_ref, saved_ref, first_ref, out_ref):
    for t in range(months):
        total = saved_ref[t, 0].astype(f32) * par_ref[MAT, 0]
        for a in range(1, ages):
            total = total + saved_ref[t, a].astype(f32) * par_ref[MAT, a]
        out_ref[t] = total
    youngest = (pos_ref[0] == 0).astype(f32)
    out_ref[months] = first_ref[...] * youngest


def spawn_parts(pos, par, saved, first):
    months, ages, rows, cols = saved.shape
    step = 16
    return pl.pallas_call(
        functools.partial(spawn_kernel, months, ages),
        grid=(rows // step,),
        in_specs=[
            whole(SMEM),
            whole(SMEM),
            pl.BlockSpec((months, ages, step, cols), lambda i: (0, 0, i, 0)),
            pl.BlockSpec((step, cols), lambda i: (i, 0)),
        ],
        out_specs=pl.BlockSpec((months + 1, step, cols), lambda i: (0, i, 0)),
        out_shape=jax.ShapeDtypeStruct((months + 1, rows, cols), f32),
        compiler_params=params_of(24),
        name="spawn_parts",
    )(pos, par, saved, first)


def sum_over(x, axis):
    n = lax.axis_size(axis)
    if n & (n - 1):
        return [x] + [shift(x, axis, d) for d in range(1, n)]
    terms = [x]
    reach = 1
    while reach < n:
        mine = functools.reduce(jnp.add, terms)
        terms = [mine, lax.ppermute(mine, axis, [(i, i ^ reach) for i in range(n)])]
        reach *= 2
    return terms


def pack_kernel(months, ages, sizes, fleets, *refs):
    pos_ref, fin_ref, next_ref, sea_ref, prey_ref, heat_ref = refs[:6]
    fleet_refs = refs[6 : 6 + fleets]
    ahead_ref, back_ref, east_ref, west_ref, both_ref, fleet_out, later_ref = refs[6 + fleets :]
    n_coh, n_lat, n_lon = sizes
    rows, cols = next_ref.shape
    keep = (pos_ref[0] < n_coh - 1).astype(f32)
    last = next_ref[...] * keep
    later_ref[...] = last

    count = fleet_refs[0].shape[0]
    half = count * fleets // 2
    for k, ref in enumerate(fleet_refs):
        at = k * count
        if count <= half:
            side, line = divmod(at, half)
            fleet_out[line : line + count, side * LANES : (side + 1) * LANES] = ref[...]
        else:
            fleet_out[0:half, 0:LANES] = ref[0:half, :]
            fleet_out[0:half, LANES : 2 * LANES] = ref[half:, :]

    band = 16
    for a in range(ages):
        if a + 1 < ages:
            top = fin_ref[a + 1, 0:band, :].astype(f32)[0:1]
            bottom = fin_ref[a + 1, rows - band : rows, :].astype(f32)[band - 1 : band]
        else:
            top, bottom = last[0:1], last[rows - 1 : rows]
        back_ref[a : a + 1, :] = top
        ahead_ref[a : a + 1, :] = bottom
    fields = [sea_ref[...].astype(f32)]
    for t in range(months):
        fields += [prey_ref[t], heat_ref[t]]
    for k, field in enumerate(fields):
        back_ref[ages + k : ages + k + 1, :] = field[0:1]
        ahead_ref[ages + k : ages + k + 1, :] = field[rows - 1 : rows]
    blank = jnp.zeros((1, cols), f32)
    start = up_to(ages + len(fields), SUB)
    for k in range(ages + len(fields), start):
        back_ref[k : k + 1, :] = blank
        ahead_ref[k : k + 1, :] = blank
    back_ref[start:, 0 : 2 * LANES] = fleet_out[...]
    ahead_ref[start:, 0 : 2 * LANES] = fleet_out[...]

    lane = lax.broadcasted_iota(jnp.int32, (rows, LANES), 1)
    east = jnp.zeros((rows, LANES), f32)
    west = jnp.zeros((rows, LANES), f32)
    for k in range(ages + len(fields)):
        if k + 1 < ages:
            left = fin_ref[k + 1, :, 0:LANES].astype(f32)
            right = fin_ref[k + 1, :, cols - LANES : cols].astype(f32)
        else:
            plane = last if k + 1 == ages else fields[k - ages]
            left, right = plane[:, 0:LANES], plane[:, cols - LANES : cols]
        west = jnp.where(lane == k, pltpu.roll(left, k, 1) if k else left, west)
        east = jnp.where(lane == k, pltpu.roll(right, k + 1, 1), east)
    east_ref[...] = east
    west_ref[...] = west
    both_ref[...] = jnp.where(pos_ref[2] == 0, east, west)


def pack_edges(sizes, pos, fin, nxt, sea, prey, heat, fleet_blocks):
    ages, rows, cols = fin.shape
    months = prey.shape[0]
    half = len(fleet_blocks) * fleet_blocks[0].shape[0] // 2
    tall = up_to(ages + 1 + 2 * months, SUB) + half
    line = jax.ShapeDtypeStruct((tall, cols), f32)
    column = jax.ShapeDtypeStruct((rows, LANES), f32)
    return pl.pallas_call(
        functools.partial(pack_kernel, months, ages, sizes, len(fleet_blocks)),
        in_specs=[whole(SMEM)] + [whole()] * (5 + len(fleet_blocks)),
        out_specs=[whole()] * 7,
        out_shape=[
            line,
            line,
            column,
            column,
            column,
            jax.ShapeDtypeStruct((half, 2 * LANES), f32),
            jax.ShapeDtypeStruct((rows, cols), f32),
        ],
        compiler_params=params_of(16),
        name="pack_edges",
    )(pos, fin, nxt, sea, prey, heat, *fleet_blocks)


def recruit_kernel(months, month, ages, sizes, terms, *refs):
    pos_ref, parv_ref, sea_ref, yield_ref, nxt_ref = refs[:5]
    term_refs = refs[5 : 5 + terms]
    rest = refs[5 + terms :]
    top_ref, bottom_ref, west_ref, east_ref = rest[:4]
    ahead_out, back_out, east_out, west_out, both_out, recruit_out, last_out = rest[4:]
    n_coh = sizes[0]
    rows, cols = sea_ref.shape
    keep = (pos_ref[0] < n_coh - 1).astype(f32)
    spawning = functools.reduce(jnp.add, [r[month] for r in term_refs])
    first = functools.reduce(jnp.add, [r[months] for r in term_refs])
    ratio = 1.0 / (1.0 + spawning)
    recruit = first * sea_ref[...].astype(f32) * yield_ref[...] * ratio * ratio
    recruit_out[...] = recruit
    mat_next = nxt_ref[rows : rows + 1, :]
    last = (nxt_ref[0:rows, :] + recruit * mat_next) * keep
    last_out[...] = last

    mat_row = parv_ref[MAT : MAT + 1, :]
    down = lax.broadcasted_iota(jnp.int32, (ages, LANES), 0)
    across = lax.broadcasted_iota(jnp.int32, (ages, LANES), 1)
    mat_col = jnp.sum(
        jnp.where(down == across, jnp.broadcast_to(mat_row, (ages, LANES)), 0.0), axis=1, keepdims=True
    )
    for src, dst, row in ((top_ref, back_out, 0), (bottom_ref, ahead_out, rows - 1)):
        full = jnp.concatenate([src[j] for j in range(src.shape[0])], axis=1)
        full = full + recruit[row : row + 1, :] * mat_col
        up = pltpu.roll(full, ages - 1, 0)
        place = lax.broadcasted_iota(jnp.int32, (ages, cols), 0)
        dst[...] = jnp.where(place == ages - 1, last[row : row + 1, :], up)
    lane = lax.broadcasted_iota(jnp.int32, (rows, LANES), 1)
    sides = []
    for src, dst, col in ((west_ref, west_out, 0), (east_ref, east_out, cols - 1)):
        full = src[...] + recruit[:, col : col + 1] * mat_row
        up = pltpu.roll(full, LANES - 1, 1)
        sides.append(jnp.where(lane == ages - 1, last[:, col : col + 1], up))
        dst[...] = sides[-1]
    both_out[...] = jnp.where(pos_ref[2] == 0, sides[1], sides[0])


def recruit_edges(sizes, month, pos, parv, sea, yields, nxt, terms, edges):
    rows, cols = sea.shape
    ages = edges[0].shape[1]
    months = terms[0].shape[0] - 1
    line = jax.ShapeDtypeStruct((ages, cols), f32)
    column = jax.ShapeDtypeStruct((rows, LANES), f32)
    return pl.pallas_call(
        functools.partial(recruit_kernel, months, month, ages, sizes, len(terms)),
        in_specs=[whole(SMEM)] + [whole()] * (4 + len(terms) + 4),
        out_specs=[whole()] * 7,
        out_shape=[line, line, column, column, column] + [jax.ShapeDtypeStruct((rows, cols), f32)] * 2,
        compiler_params=params_of(8),
        name="recruit_edges",
    )(pos, parv, sea, yields, nxt, *terms, *edges)


def habitat_of(forage, heat, ideal, tau):
    off = heat - ideal
    return forage * (tau / (1.0 + off * off))


def month_kernel(cfg, *refs):
    (months, month, ages, sizes, count, later_bf16, with_recruit, last_month, n_fleet, n_terms, n_bcast, edges_out) = cfg
    refs = list(refs)

    def take(n):
        out = refs[:n]
        del refs[:n]
        return out

    pos_ref, par_ref, parv_ref = take(3)
    later_ref, next_ref = take(2)
    own_ahead, own_back, own_east, own_west = take(4)
    from_before, from_after, from_west, from_east = take(4)
    if with_recruit:
        msg_before, msg_after, msg_west, msg_east = take(4)
        (recruit_ref,) = take(1)
    else:
        msg_before, msg_after, msg_west, msg_east = from_before, from_after, from_west, from_east
    sea_ref, prey_ref, heat_ref, fish_ref = take(4)
    fleet_refs = take(n_fleet)
    if last_month:
        (yield_ref,) = take(1)
        term_refs = take(n_terms)
        bcast_refs = take(n_bcast)
        out_ref, grad_ref = take(2)
    elif edges_out:
        out_ref, top_out, bottom_out, west_out, east_out = take(5)
    else:
        (out_ref,) = take(1)
    openv, openh, forage, heat4, rowc, colw, cole, catch = take(8)
    if last_month:
        (final_recruit,) = take(1)

    n_coh, n_lat, n_lon = sizes
    rows, cols = sea_ref.shape
    n_i, n_j = rows // SUB, cols // LANES
    blocks_y, blocks_x = rows // BY, cols // BX
    sea_line, prey_line, heat_line = ages, ages + 1 + 2 * month, ages + 2 + 2 * month
    step = pl.program_id(0)

    @pl.when(step == 0)
    def _():
        sea = sea_ref[...].astype(f32)
        line = lax.broadcasted_iota(jnp.int32, (rows, cols), 0)
        column = lax.broadcasted_iota(jnp.int32, (rows, cols), 1)
        openv[...] = jnp.where(line == rows - 1, 0.0, sea * pltpu.roll(sea, rows - 1, 0))
        openh[...] = jnp.where(column == cols - 1, 0.0, sea * pltpu.roll(sea, cols - 1, 1))
        heat_q = heat_ref[0] * 0.25
        heat4[...] = heat_q
        fields = sea * prey_ref[0]
        forage[...] = fields

        down = lax.broadcasted_iota(jnp.int32, (ages, LANES), 0)
        across = lax.broadcasted_iota(jnp.int32, (ages, LANES), 1)

        def as_column(k):
            row = jnp.broadcast_to(parv_ref[k : k + 1, :], (ages, LANES))
            return jnp.sum(jnp.where(down == across, row, 0.0), axis=1, keepdims=True)

        kappa, tau, ideal = as_column(KAPPA), as_column(TAU), as_column(IDEAL)
        has = [
            (pos_ref[1] > 0).astype(f32),
            (pos_ref[1] < n_lat - 1).astype(f32),
            (pos_ref[2] > 0).astype(f32),
            (pos_ref[2] < n_lon - 1).astype(f32),
        ]
        for k, (row, own, got, msg) in enumerate(
            ((0, own_back, from_before, msg_before), (rows - 1, own_ahead, from_after, msg_after))
        ):
            here = habitat_of(fields[row : row + 1], heat_q[row : row + 1], ideal, tau)
            sea_there = msg[sea_line : sea_line + 1, :]
            there = habitat_of(
                sea_there * msg[prey_line : prey_line + 1, :], msg[heat_line : heat_line + 1, :] * 0.25, ideal, tau
            )
            rate = (sea[row : row + 1] * sea_there * has[k]) * (kappa + jnp.maximum(there - here, 0.0))
            flux = rate * (own[0:ages, :] - got[0:ages, :])
            for j in range(n_j):
                rowc[k, j] = flux[:, j * LANES : (j + 1) * LANES]
        kappa, tau, ideal = parv_ref[KAPPA : KAPPA + 1], parv_ref[TAU : TAU + 1], parv_ref[IDEAL : IDEAL + 1]
        for k, (col, own, got, msg, dst) in enumerate(
            ((0, own_west, from_west, msg_west, colw), (cols - 1, own_east, from_east, msg_east, cole))
        ):
            here = habitat_of(fields[:, col : col + 1], heat_q[:, col : col + 1], ideal, tau)
            sea_there = msg[:, sea_line : sea_line + 1]
            there = habitat_of(
                sea_there * msg[:, prey_line : prey_line + 1], msg[:, heat_line : heat_line + 1] * 0.25, ideal, tau
            )
            rate = (sea[:, col : col + 1] * sea_there * has[2 + k]) * (kappa + jnp.maximum(there - here, 0.0))
            dst[...] = rate * (own[...] - got[...])

        flat = []
        for ref in fleet_refs:
            flat += [ref[:, 0:LANES], ref[:, LANES : 2 * LANES]]
        flat = jnp.concatenate(flat, axis=0)
        names = flat[:, 2 * ages : 2 * ages + 1] if months == 2 else flat[:, months * ages : months * ages + 1]
        turned = flat.T[month * ages : (month + 1) * ages]
        base = ((pos_ref[1] * n_lon + pos_ref[2]) * (blocks_y * blocks_x)).astype(f32)
        block_col = (lax.broadcasted_iota(jnp.int32, (flat.shape[0], cols), 1) // BX).astype(f32)
        gear = as_column(GEAR)
        for by in range(blocks_y):
            named = (block_col == names - (base + by * blocks_x)).astype(f32)
            sums = gear * jnp.dot(turned, named, precision=lax.Precision.HIGHEST, preferred_element_type=f32)
            for j in range(n_j):
                catch[by, j] = sums[:, j * LANES : (j + 1) * LANES]

        if last_month:
            totals = [functools.reduce(jnp.add, [r[t] for r in term_refs]) for t in range(months + 1)]
            own = bcast_refs[0][...]
            wrapped = bcast_refs[1][...]
            first = own * (pos_ref[0] == 0).astype(f32) + wrapped * (pos_ref[0] == n_coh - 1).astype(f32)
            for ref in bcast_refs[2:]:
                first = first + ref[...]
            first = first[0:rows] + recruit_ref[...] * first[rows : rows + 1]
            ratios = [1.0 / (1.0 + totals[t]) for t in range(months)]
            grad_ref[...] = (totals[months] * totals[1] * ratios[1] + first * totals[0] * ratios[0]) * sea
            final_recruit[...] = first * sea * yield_ref[...] * ratios[0] * ratios[0]

    lane = lax.broadcasted_iota(jnp.int32, (SUB, LANES), 1)
    sub = lax.broadcasted_iota(jnp.int32, (SUB, LANES), 0)

    def tile(i, j):
        return slice(i * SUB, (i + 1) * SUB), slice(j * LANES, (j + 1) * LANES)

    def cohort(k, load):
        a = step * count + k
        kappa, tau, ideal = par_ref[KAPPA, a], par_ref[TAU, a], par_ref[IDEAL, a]
        death, gear2 = par_ref[DEATH, a], par_ref[GEAR2, a]
        if last_month:
            mat = par_ref[MAT, a]
        if with_recruit:
            mat_later = par_ref[MAT, a + 1]

        def strip(i):
            adj, hab = [], []
            for j in range(n_j):
                at = tile(i, j)
                value = load(*at)
                if with_recruit and load is not load_next:
                    value = value + recruit_ref[at] * mat_later
                adj.append(value)
                off = heat4[at] - ideal
                hab.append(forage[at] * tau * pl.reciprocal(1.0 + off * off, approx=False))
            return adj, hab, [pltpu.roll(v, SUB - 1, 0) for v in adj], [pltpu.roll(v, SUB - 1, 0) for v in hab]

        now = strip(0)
        above = [jnp.broadcast_to(-rowc[0, j, pl.ds(a, 1), :], (SUB, LANES)) for j in range(n_j)]
        below = [jnp.broadcast_to(rowc[1, j, pl.ds(a, 1), :], (SUB, LANES)) for j in range(n_j)]
        for i in range(n_i):
            after = strip(i + 1) if i + 1 < n_i else now
            adj, hab, adj_up, hab_up = now
            out = [None] * n_j
            for j in range(n_j):
                at = tile(i, j)
                adj_d = jnp.where(sub == SUB - 1, after[2][j], adj_up[j])
                hab_d = jnp.where(sub == SUB - 1, after[3][j], hab_up[j])
                g = hab_d - hab[j]
                d = openv[at] * (adj[j] - adj_d)
                p = jnp.maximum(g, 0.0) + kappa
                f = p * d
                if i == n_i - 1:
                    f = jnp.where(sub == SUB - 1, below[j], f)
                turned = pltpu.roll((p - g) * d, 1, 0)
                out[j] = f - jnp.where(sub == 0, above[j], turned)
                above[j] = turned
            adj_l = [pltpu.roll(v, LANES - 1, 1) for v in adj]
            hab_l = [pltpu.roll(v, LANES - 1, 1) for v in hab]
            flows, backs = [], []
            for j in range(n_j):
                at = tile(i, j)
                if j + 1 < n_j:
                    adj_d = jnp.where(lane == LANES - 1, adj_l[j + 1], adj_l[j])
                    hab_d = jnp.where(lane == LANES - 1, hab_l[j + 1], hab_l[j])
                else:
                    adj_d, hab_d = adj_l[j], hab_l[j]
                g = hab_d - hab[j]
                d = openh[at] * (adj[j] - adj_d)
                p = jnp.maximum(g, 0.0) + kappa
                flows.append(p * d)
                backs.append(pltpu.roll((p - g) * d, 1, 1))
            rs = slice(i * SUB, (i + 1) * SUB)
            edge_e = pltpu.roll(cole[rs, :], (2 * LANES - 1) - a, 1)
            edge_w = pltpu.roll(-colw[rs, :], LANES - a, 1)
            flows[-1] = jnp.where(lane == LANES - 1, edge_e, flows[-1])
            for j in range(n_j):
                at = tile(i, j)
                came = jnp.where(lane == 0, backs[j - 1] if j else edge_w, backs[j])
                moved = adj[j] - (out[j] + flows[j] - came)
                fish = fish_ref[at]
                survive = jnp.exp2(death - gear2 * fish)
                caught = catch[i * SUB // BY, j, pl.ds(a, 1), :]
                value = survive * moved + fish * caught
                if last_month:
                    value = value + final_recruit[at] * mat
                out_ref[(k,) + at] = value
                if edges_out:
                    if i == 0:
                        top_out[j, pl.ds(a, 1), :] = value[0:1]
                    if i == n_i - 1:
                        bottom_out[j, pl.ds(a, 1), :] = value[SUB - 1 : SUB]
                    if j == 0:
                        west_out[rs, :] = jnp.where(lane == a, pltpu.roll(value, a, 1), west_out[rs, :])
                    if j == n_j - 1:
                        east_out[rs, :] = jnp.where(lane == a, pltpu.roll(value, a + 1, 1), east_out[rs, :])
            now = after

    def load_next(ys, xs):
        return next_ref[ys, xs]

    def loader(a):
        def load(ys, xs):
            if later_bf16:
                low = ys.start // 16 * 16
                wide = later_ref[a + 1, low : low + 16, xs].astype(f32)
                return wide[ys.start - low : ys.stop - low]
            return later_ref[a + 1, ys, xs]

        return load

    if count == 1:
        cohort(0, loader(0))
    else:
        if edges_out:
            @pl.when(step == 0)
            def _():
                west_out[...] = jnp.zeros_like(west_out)
                east_out[...] = jnp.zeros_like(east_out)

        final_step = step == ages // count - 1

        def body(k, carry):
            cohort(k, loader(step * count + k))
            return carry

        lax.fori_loop(0, jnp.where(final_step, count - 1, count), body, 0)

        @pl.when(final_step)
        def _():
            cohort(count - 1, load_next)


def month_step(
    sizes, month, months, pos, par, parv, later, nxt, own, got, first_got, recruit, sea, prey, heat, fish,
    fleet_blocks, first_only=False, final=None
):
    ages, rows, cols = later.shape
    later_bf16 = later.dtype == jnp.bfloat16
    with_recruit = recruit is not None
    count = 1 if first_only else GROUP
    last_month = final is not None
    edges_out = not last_month and not first_only
    line = jax.ShapeDtypeStruct((cols // LANES, ages, LANES), f32)
    column = jax.ShapeDtypeStruct((rows, LANES), f32)
    fleet_specs = []
    fleet_args = []
    for block, start in fleet_blocks:
        size = block.shape[0] - start
        fleet_args.append(block)
        fleet_specs.append((start, size))
    operands = [pos, par, parv, later, nxt, *own, *got]
    if with_recruit:
        operands += [*first_got, recruit]
    specs = [whole(SMEM), whole(SMEM)] + [whole()] * (len(operands) - 2)
    operands += [sea, prey, heat, fish]
    one = pl.BlockSpec((1, rows, cols), lambda i: (month, 0, 0))
    specs += [whole(), one, one, whole()]
    operands += fleet_args
    specs += [whole()] * len(fleet_args)
    n_terms = n_bcast = 0
    if last_month:
        yields, terms, bcasts = final
        operands += [yields, *terms, *bcasts]
        specs += [whole()] * (1 + len(terms) + len(bcasts))
        n_terms, n_bcast = len(terms), len(bcasts)
    if first_only:
        out_shape = [jax.ShapeDtypeStruct((1, rows, cols), f32)]
        out_specs = [pl.BlockSpec((1, rows, cols), lambda i: (0, 0, 0))]
        grid = (1,)
    else:
        out_shape = [jax.ShapeDtypeStruct((ages, rows, cols), f32)]
        out_specs = [pl.BlockSpec((count, rows, cols), lambda i: (i, 0, 0))]
        grid = (ages // count,)
    if last_month:
        out_shape.append(jax.ShapeDtypeStruct((rows, cols), f32))
        out_specs.append(whole())
    elif edges_out:
        out_shape += [line, line, column, column]
        out_specs += [whole()] * 4
    scratch = [
        pltpu.VMEM((rows, cols), f32),
        pltpu.VMEM((rows, cols), f32),
        pltpu.VMEM((rows, cols), f32),
        pltpu.VMEM((rows, cols), f32),
        pltpu.VMEM((2, cols // LANES, ages, LANES), f32),
        pltpu.VMEM((rows, LANES), f32),
        pltpu.VMEM((rows, LANES), f32),
        pltpu.VMEM((rows // BY, cols // LANES, ages, LANES), f32),
    ]
    if last_month:
        scratch.append(pltpu.VMEM((rows, cols), f32))
    cfg = (
        months, month, ages, sizes, count, later_bf16, with_recruit, last_month, len(fleet_args), n_terms, n_bcast,
        edges_out,
    )

    def kernel(*refs):
        refs = list(refs)
        at = len(operands) - (0 if not last_month else 1 + n_terms + n_bcast) - len(fleet_args)
        for k, (start, size) in enumerate(fleet_specs):
            if start:
                refs[at + k] = refs[at + k].at[start : start + size]
        month_kernel(cfg, *refs)

    cells = (1 if first_only else ages) * rows * cols
    return pl.pallas_call(
        kernel,
        grid=grid,
        in_specs=specs,
        out_specs=out_specs,
        out_shape=out_shape,
        scratch_shapes=scratch,
        cost_estimate=pl.CostEstimate(flops=60 * cells, bytes_accessed=8 * cells, transcendentals=2 * cells),
        compiler_params=params_of(24),
        name="month_first" if first_only else "month_step",
    )(*operands)


def shards(
    saved,
    fin,
    prey,
    heat,
    sea,
    fish,
    yields,
    death,
    gear,
    kappa,
    tau,
    ideal,
    breeding,
    landing,
    east_piece,
    north_piece,
    patch,
    bounds,
):
    months, ages, rows, cols = saved.shape
    n_coh, n_lat, n_lon = sizes = tuple(lax.axis_size(axis) for axis in ("coh", "lat", "lon"))
    at_coh, at_lat, at_lon = (lax.axis_index(axis) for axis in ("coh", "lat", "lon"))
    pos = jnp.stack([at_coh, at_lat, at_lon]).astype(jnp.int32)
    cohort_age = at_coh * ages + jnp.arange(ages)
    maturity = (cohort_age + 1).astype(f32) / (ages * n_coh) * breeding
    table = jnp.stack([death * -LOG2E, gear * LOG2E, kappa, tau, ideal * 0.25, maturity, gear, gear])
    par = jnp.pad(table, ((0, 0), (0, LANES - ages)))

    nblocks = (rows // BY) * (cols // BX)
    inside = (cohort_age[None, :] >= bounds[:, 0:1]) & (cohort_age[None, :] < bounds[:, 1:2])
    masked = (landing * inside[:, None, :].astype(f32)).reshape(landing.shape[0], months * ages)
    names = ((north_piece * n_lon + east_piece[:, 0]) * nblocks + patch).astype(f32)
    fleet = jnp.concatenate([masked, names[:, None]], axis=1)
    fleet = jnp.pad(fleet, ((0, 0), (0, LANES - fleet.shape[1])))

    first = fin[0].astype(f32)
    nxt = shift(first, "coh", -1)
    fleet_lon = [fleet] + [shift(fleet, "lon", d) for d in range(1, n_lon)]
    terms = sum_over(spawn_parts(pos, par, saved, first), "coh")

    ahead, back, east, west, both, fleet_pack, later_last = pack_edges(
        sizes, pos, fin, nxt, sea, prey, heat, fleet_lon
    )
    from_west, from_east = swap_edges(east, west, both, "lon")
    from_before, from_after = shift(ahead, "lat", 1), shift(back, "lat", -1)
    start = ahead.shape[0] - fleet_pack.shape[0]
    fleet_blocks = [(ahead, start), (from_before, start)]
    if n_lat > 2:
        fleet_blocks.append((from_after, start))
    fleet_blocks += [(shift(fleet_pack, "lat", d), 0) for d in range(2, n_lat - 1)]

    own = (ahead, back, east, west)
    got = first_got = (from_before, from_after, from_west, from_east)
    later, nxt, recruit = fin, later_last, None
    for month in range(months - 1, 0, -1):
        common = (sizes, month, months, pos, par, par, later, nxt, own, got, first_got, recruit, sea, prey, heat, fish)
        (plane,) = month_step(*common, fleet_blocks, first_only=True)
        mat_rows = jnp.broadcast_to(maturity[0], (SUB, cols))
        plane = jnp.concatenate([plane[0], mat_rows], axis=0)
        down = shift(plane, "coh", -1)
        bcasts = [plane, down] + [lax.ppermute(plane, "coh", [(0, j)]) for j in range(1, n_coh - 1)]
        later, *edges = month_step(*common, fleet_blocks)
        ahead, back, east, west, both, recruit, nxt = recruit_edges(
            sizes, month, pos, par, sea, yields, down, terms, edges
        )
        own = (ahead, back, east, west)
        got = (
            shift(ahead, "lat", 1),
            shift(back, "lat", -1),
            *swap_edges(east, west, both, "lon"),
        )
    return tuple(month_step(
        sizes, 0, months, pos, par, par, later, nxt, own, got, first_got, recruit, sea, prey, heat, fish,
        fleet_blocks, final=(yields, terms, bcasts)
    ))


def solution(mesh):
    in_specs = (
        P(None, "coh", "lat", "lon"),
        P("coh", "lat", "lon"),
        P(None, "lat", "lon"),
        P(None, "lat", "lon"),
        P("lat", "lon"),
        P("lat", "lon"),
        P("lat", "lon"),
        P("coh"),
        P("coh"),
        P("coh"),
        P("coh"),
        P("coh"),
        P("coh"),
        P(("lat", "lon"), None, "coh"),
        P(("lat", "lon"), None),
        P(("lat", "lon")),
        P(("lat", "lon")),
        P(("lat", "lon"), None),
    )
    out_specs = (P("coh", "lat", "lon"), P("lat", "lon"))

    return jax.shard_map(shards, mesh=mesh, in_specs=in_specs, out_specs=out_specs, check_vma=False)
```

```python
import functools
import math

import jax
import jax.numpy as jnp
from jax import lax
from jax.experimental import pallas as pl
from jax.experimental.pallas import tpu as pltpu
from jax.sharding import PartitionSpec as P

BY = 16
BX = 32
LANES = 128
SUB = 8
GROUP = 8
PAIR = 2
SPAWN_MB = 24

f32 = jnp.float32
VMEM = pltpu.MemorySpace.VMEM
SMEM = pltpu.MemorySpace.SMEM
LOG2E = math.log2(math.e)

DEATH, GEAR2, KAPPA, TAU, IDEAL, MAT, GEAR = range(7)


def up_to(value, step):
    return -(-value // step) * step


def whole(memory=VMEM):
    return pl.BlockSpec(memory_space=memory)


def params_of(limit=48):
    return pltpu.CompilerParams(vmem_limit_bytes=limit * 2**20)


def shift(x, axis, distance):
    n = lax.axis_size(axis)
    return lax.ppermute(x, axis, [(i, (i + distance) % n) for i in range(n)])


def swap_edges(ahead, back, both, axis):
    n = lax.axis_size(axis)
    if n == 1:
        return ahead, back
    if n == 2:
        got = shift(both, axis, 1)
        return got, got
    return shift(ahead, axis, 1), shift(back, axis, -1)


def spawn_kernel(months, ages, total_ages, pos_ref, breed_ref, saved_ref, first_ref, _, out_ref):
    mat = [(pos_ref[0] * ages + (a + 1)).astype(f32) / total_ages * breed_ref[a] for a in range(ages)]
    for t in range(months):
        total = saved_ref[t, 0].astype(f32) * mat[0]
        for a in range(1, ages):
            total = total + saved_ref[t, a].astype(f32) * mat[a]
        out_ref[t] = total
    youngest = (pos_ref[0] == 0).astype(f32)
    out_ref[months] = first_ref[...] * youngest


def spawn_parts(pos, breeding, total_ages, saved, first, ahead_of):
    months, ages, rows, cols = saved.shape
    step = 16
    return pl.pallas_call(
        functools.partial(spawn_kernel, months, ages, total_ages),
        grid=(rows // step,),
        in_specs=[
            whole(SMEM),
            whole(SMEM),
            pl.BlockSpec((months, ages, step, cols), lambda i: (0, 0, i, 0)),
            pl.BlockSpec((step, cols), lambda i: (i, 0)),
            pl.BlockSpec(memory_space=pl.ANY),
        ],
        out_specs=pl.BlockSpec((months + 1, step, cols), lambda i: (0, i, 0)),
        out_shape=jax.ShapeDtypeStruct((months + 1, rows, cols), f32),
        compiler_params=params_of(SPAWN_MB),
        name="spawn_parts",
    )(pos, breeding, saved, first, ahead_of)


def add_kernel(a_ref, b_ref, _, out_ref):
    out_ref[...] = a_ref[...] + b_ref[...]


def add_after(a, b, ahead_of):
    return pl.pallas_call(
        add_kernel,
        in_specs=[whole(), whole(), pl.BlockSpec(memory_space=pl.ANY)],
        out_specs=whole(),
        out_shape=jax.ShapeDtypeStruct(a.shape, a.dtype),
        compiler_params=params_of(8),
        name="add_after",
    )(a, b, ahead_of)


def flipped(x, axis, reach):
    return lax.ppermute(x, axis, [(i, i ^ reach) for i in range(lax.axis_size(axis))])


def first_terms(x, axis):
    n = lax.axis_size(axis)
    if n & (n - 1):
        return [x] + [shift(x, axis, d) for d in range(1, n)]
    return [x, flipped(x, axis, 1)] if n > 1 else [x]


def other_terms(terms, axis, ahead_of):
    n = lax.axis_size(axis)
    if n & (n - 1):
        return terms
    reach = 2
    while reach < n:
        mine = add_after(*terms, ahead_of)
        terms = [mine, flipped(mine, axis, reach)]
        reach *= 2
    return terms


def pack_kernel(months, ages, sizes, fleets, *refs):
    pos_ref, fin_ref, next_ref, sea_ref, prey_ref, heat_ref = refs[:6]
    fleet_refs = refs[6 : 6 + fleets]
    death_ref, gear_ref, kappa_ref, tau_ref, ideal_ref, breed_ref = refs[6 + fleets : 12 + fleets]
    ahead_ref, back_ref, east_ref, west_ref, both_ref, fleet_out, later_ref, table_ref = refs[12 + fleets :]
    n_coh, n_lat, n_lon = sizes
    age = lax.broadcasted_iota(jnp.int32, (1, ages), 1) + (pos_ref[0] * ages + 1)
    table_ref[...] = jnp.zeros_like(table_ref)
    table_ref[DEATH : DEATH + 1, 0:ages] = death_ref[...] * -LOG2E
    table_ref[GEAR2 : GEAR2 + 1, 0:ages] = gear_ref[...] * LOG2E
    table_ref[KAPPA : KAPPA + 1, 0:ages] = kappa_ref[...]
    table_ref[TAU : TAU + 1, 0:ages] = tau_ref[...]
    table_ref[IDEAL : IDEAL + 1, 0:ages] = ideal_ref[...] * 0.25
    table_ref[MAT : MAT + 1, 0:ages] = age.astype(f32) / (ages * n_coh) * breed_ref[...]
    table_ref[GEAR : GEAR + 1, 0:ages] = gear_ref[...]
    rows, cols = next_ref.shape
    keep = (pos_ref[0] < n_coh - 1).astype(f32)
    last = next_ref[...] * keep
    later_ref[...] = last

    count = fleet_refs[0].shape[0]
    half = count * fleets // 2
    for k, ref in enumerate(fleet_refs):
        at = k * count
        if count <= half:
            side, line = divmod(at, half)
            fleet_out[line : line + count, side * LANES : (side + 1) * LANES] = ref[...]
        else:
            fleet_out[0:half, 0:LANES] = ref[0:half, :]
            fleet_out[0:half, LANES : 2 * LANES] = ref[half:, :]

    band = 16
    for a in range(ages):
        if a + 1 < ages:
            top = fin_ref[a + 1, 0:band, :].astype(f32)[0:1]
            bottom = fin_ref[a + 1, rows - band : rows, :].astype(f32)[band - 1 : band]
        else:
            top, bottom = last[0:1], last[rows - 1 : rows]
        back_ref[a : a + 1, :] = top
        ahead_ref[a : a + 1, :] = bottom
    fields = [sea_ref[...].astype(f32)]
    for t in range(months):
        fields += [prey_ref[t], heat_ref[t]]
    for k, field in enumerate(fields):
        back_ref[ages + k : ages + k + 1, :] = field[0:1]
        ahead_ref[ages + k : ages + k + 1, :] = field[rows - 1 : rows]
    blank = jnp.zeros((1, cols), f32)
    start = up_to(ages + len(fields), SUB)
    for k in range(ages + len(fields), start):
        back_ref[k : k + 1, :] = blank
        ahead_ref[k : k + 1, :] = blank
    back_ref[start:, 0 : 2 * LANES] = fleet_out[...]
    ahead_ref[start:, 0 : 2 * LANES] = fleet_out[...]

    lane = lax.broadcasted_iota(jnp.int32, (rows, LANES), 1)
    east = jnp.zeros((rows, LANES), f32)
    west = jnp.zeros((rows, LANES), f32)
    for k in range(ages + len(fields)):
        if k + 1 < ages:
            left = fin_ref[k + 1, :, 0:LANES].astype(f32)
            right = fin_ref[k + 1, :, cols - LANES : cols].astype(f32)
        else:
            plane = last if k + 1 == ages else fields[k - ages]
            left, right = plane[:, 0:LANES], plane[:, cols - LANES : cols]
        west = jnp.where(lane == k, pltpu.roll(left, k, 1) if k else left, west)
        east = jnp.where(lane == k, pltpu.roll(right, k + 1, 1), east)
    east_ref[...] = east
    west_ref[...] = west
    both_ref[...] = jnp.where(pos_ref[2] == 0, east, west)


def pack_edges(sizes, pos, fin, nxt, sea, prey, heat, fleet_blocks, rates):
    ages, rows, cols = fin.shape
    months = prey.shape[0]
    half = len(fleet_blocks) * fleet_blocks[0].shape[0] // 2
    tall = up_to(ages + 1 + 2 * months, SUB) + half
    line = jax.ShapeDtypeStruct((tall, cols), f32)
    column = jax.ShapeDtypeStruct((rows, LANES), f32)
    return pl.pallas_call(
        functools.partial(pack_kernel, months, ages, sizes, len(fleet_blocks)),
        in_specs=[whole(SMEM)] + [whole()] * (5 + len(fleet_blocks) + len(rates)),
        out_specs=[whole()] * 8,
        out_shape=[
            line,
            line,
            column,
            column,
            column,
            jax.ShapeDtypeStruct((half, 2 * LANES), f32),
            jax.ShapeDtypeStruct((rows, cols), f32),
            jax.ShapeDtypeStruct((SUB, LANES), f32),
        ],
        compiler_params=params_of(16),
        name="pack_edges",
    )(pos, fin, nxt, sea, prey, heat, *fleet_blocks, *[rate.reshape(1, ages) for rate in rates])


def recruit_kernel(months, month, ages, sizes, terms, *refs):
    pos_ref, parv_ref, sea_ref, yield_ref, nxt_ref = refs[:5]
    term_refs = refs[5 : 5 + terms]
    rest = refs[5 + terms :]
    top_ref, bottom_ref, west_ref, east_ref = rest[:4]
    ahead_out, back_out, east_out, west_out, both_out, recruit_out, last_out = rest[4:]
    n_coh = sizes[0]
    rows, cols = sea_ref.shape
    keep = (pos_ref[0] < n_coh - 1).astype(f32)
    spawning = functools.reduce(jnp.add, [r[month] for r in term_refs])
    first = functools.reduce(jnp.add, [r[months] for r in term_refs])
    ratio = 1.0 / (1.0 + spawning)
    recruit = first * sea_ref[...].astype(f32) * yield_ref[...] * ratio * ratio
    recruit_out[...] = recruit
    mat_next = nxt_ref[rows : rows + 1, :]
    last = (nxt_ref[0:rows, :] + recruit * mat_next) * keep
    last_out[...] = last

    mat_row = parv_ref[MAT : MAT + 1, :]
    down = lax.broadcasted_iota(jnp.int32, (ages, LANES), 0)
    across = lax.broadcasted_iota(jnp.int32, (ages, LANES), 1)
    mat_col = jnp.sum(
        jnp.where(down == across, jnp.broadcast_to(mat_row, (ages, LANES)), 0.0), axis=1, keepdims=True
    )
    for src, dst, row in ((top_ref, back_out, 0), (bottom_ref, ahead_out, rows - 1)):
        full = jnp.concatenate([src[j] for j in range(src.shape[0])], axis=1)
        full = full + recruit[row : row + 1, :] * mat_col
        up = pltpu.roll(full, ages - 1, 0)
        place = lax.broadcasted_iota(jnp.int32, (ages, cols), 0)
        dst[...] = jnp.where(place == ages - 1, last[row : row + 1, :], up)
    lane = lax.broadcasted_iota(jnp.int32, (rows, LANES), 1)
    sides = []
    for src, dst, col in ((west_ref, west_out, 0), (east_ref, east_out, cols - 1)):
        full = src[...] + recruit[:, col : col + 1] * mat_row
        up = pltpu.roll(full, LANES - 1, 1)
        sides.append(jnp.where(lane == ages - 1, last[:, col : col + 1], up))
        dst[...] = sides[-1]
    both_out[...] = jnp.where(pos_ref[2] == 0, sides[1], sides[0])


def recruit_edges(sizes, month, pos, parv, sea, yields, nxt, terms, edges):
    rows, cols = sea.shape
    ages = edges[0].shape[1]
    months = terms[0].shape[0] - 1
    line = jax.ShapeDtypeStruct((ages, cols), f32)
    column = jax.ShapeDtypeStruct((rows, LANES), f32)
    return pl.pallas_call(
        functools.partial(recruit_kernel, months, month, ages, sizes, len(terms)),
        in_specs=[whole(SMEM)] + [whole()] * (4 + len(terms) + 4),
        out_specs=[whole()] * 7,
        out_shape=[line, line, column, column, column] + [jax.ShapeDtypeStruct((rows, cols), f32)] * 2,
        compiler_params=params_of(8),
        name="recruit_edges",
    )(pos, parv, sea, yields, nxt, *terms, *edges)


class Cfg:
    def __init__(self, **kw):
        self.__dict__.update(kw)


def column_of(par_ref, k, ages):
    down = lax.broadcasted_iota(jnp.int32, (ages, LANES), 0)
    across = lax.broadcasted_iota(jnp.int32, (ages, LANES), 1)
    row = jnp.broadcast_to(par_ref[k : k + 1, :], (ages, LANES))
    return jnp.sum(jnp.where(down == across, row, 0.0), axis=1, keepdims=True)


def edge_flux(c, pos_ref, parv_ref, sea_ref, forage_ref, heat4_ref, own, got, msgs, rowc, colw, cole):
    rows, cols, ages = c.rows, c.cols, c.ages
    n_coh, n_lat, n_lon = c.sizes
    own_ahead, own_back, own_east, own_west = own
    from_before, from_after, from_west, from_east = got
    msg_before, msg_after, msg_west, msg_east = msgs
    sea_line, prey_line, heat_line = ages, ages + 1 + 2 * c.month, ages + 2 + 2 * c.month
    kappa, tau, ideal = (column_of(parv_ref, k, ages) for k in (KAPPA, TAU, IDEAL))
    has = [
        (pos_ref[1] > 0).astype(f32),
        (pos_ref[1] < n_lat - 1).astype(f32),
        (pos_ref[2] > 0).astype(f32),
        (pos_ref[2] < n_lon - 1).astype(f32),
    ]
    for k, (row, own, got, msg) in enumerate(
        ((0, own_back, from_before, msg_before), (rows - 1, own_ahead, from_after, msg_after))
    ):
        here = habitat_of(forage_ref[row : row + 1, :], heat4_ref[row : row + 1, :], ideal, tau)
        sea_there = msg[sea_line : sea_line + 1, :]
        there = habitat_of(
            sea_there * msg[prey_line : prey_line + 1, :], msg[heat_line : heat_line + 1, :] * 0.25, ideal, tau
        )
        both = sea_ref[row : row + 1, :].astype(f32) * sea_there * has[k]
        flux = both * (kappa + jnp.maximum(there - here, 0.0)) * (own[0:ages, :] - got[0:ages, :])
        for j in range(cols // LANES):
            rowc[k, j] = flux[:, j * LANES : (j + 1) * LANES]
    kappa, tau, ideal = (parv_ref[k : k + 1, :] for k in (KAPPA, TAU, IDEAL))
    for k, (col, own, got, msg, dst) in enumerate(
        ((0, own_west, from_west, msg_west, colw), (cols - 1, own_east, from_east, msg_east, cole))
    ):
        here = habitat_of(forage_ref[:, col : col + 1], heat4_ref[:, col : col + 1], ideal, tau)
        sea_there = msg[:, sea_line : sea_line + 1]
        there = habitat_of(
            sea_there * msg[:, prey_line : prey_line + 1], msg[:, heat_line : heat_line + 1] * 0.25, ideal, tau
        )
        both = sea_ref[:, col : col + 1].astype(f32) * sea_there * has[2 + k]
        dst[...] = both * (kappa + jnp.maximum(there - here, 0.0)) * (own[...] - got[...])


def advance(c, k, a, par_ref, load, tables, out_ref, recruit=None, lines=None):
    openv, openh, forage, heat4, fish_ref, rowc, colw, cole, catch = tables
    n_i, n_j = c.rows // SUB, c.cols // LANES
    lane = lax.broadcasted_iota(jnp.int32, (SUB, LANES), 1)
    sub = lax.broadcasted_iota(jnp.int32, (SUB, LANES), 0)
    kappa, tau, ideal = par_ref[KAPPA, a], par_ref[TAU, a], par_ref[IDEAL, a]
    death, gear2 = par_ref[DEATH, a], par_ref[GEAR2, a]
    if recruit is not None:
        mat = par_ref[MAT, a]

    def tile(i, j):
        return slice(i * SUB, (i + 1) * SUB), slice(j * LANES, (j + 1) * LANES)

    def strip(i):
        adj, hab = [], []
        for j in range(n_j):
            at = tile(i, j)
            adj.append(load(*at))
            off = heat4[at] - ideal
            hab.append(forage[at] * tau * pl.reciprocal(1.0 + off * off, approx=False))
        return adj, hab, [pltpu.roll(v, SUB - 1, 0) for v in adj], [pltpu.roll(v, SUB - 1, 0) for v in hab]

    now = strip(0)
    above = [jnp.broadcast_to(-rowc[0, j, pl.ds(a, 1), :], (SUB, LANES)) for j in range(n_j)]
    below = [jnp.broadcast_to(rowc[1, j, pl.ds(a, 1), :], (SUB, LANES)) for j in range(n_j)]
    for i in range(n_i):
        after = strip(i + 1) if i + 1 < n_i else now
        adj, hab, adj_up, hab_up = now
        out = [None] * n_j
        for j in range(n_j):
            at = tile(i, j)
            adj_d = jnp.where(sub == SUB - 1, after[2][j], adj_up[j])
            hab_d = jnp.where(sub == SUB - 1, after[3][j], hab_up[j])
            g = hab_d - hab[j]
            d = openv[at] * (adj[j] - adj_d)
            p = jnp.maximum(g, 0.0) + kappa
            f = p * d
            if i == n_i - 1:
                f = jnp.where(sub == SUB - 1, below[j], f)
            turned = pltpu.roll((p - g) * d, 1, 0)
            out[j] = f - jnp.where(sub == 0, above[j], turned)
            above[j] = turned
        adj_l = [pltpu.roll(v, LANES - 1, 1) for v in adj]
        hab_l = [pltpu.roll(v, LANES - 1, 1) for v in hab]
        flows, backs = [], []
        for j in range(n_j):
            at = tile(i, j)
            if j + 1 < n_j:
                adj_d = jnp.where(lane == LANES - 1, adj_l[j + 1], adj_l[j])
                hab_d = jnp.where(lane == LANES - 1, hab_l[j + 1], hab_l[j])
            else:
                adj_d, hab_d = adj_l[j], hab_l[j]
            g = hab_d - hab[j]
            d = openh[at] * (adj[j] - adj_d)
            p = jnp.maximum(g, 0.0) + kappa
            flows.append(p * d)
            backs.append(pltpu.roll((p - g) * d, 1, 1))
        rs = slice(i * SUB, (i + 1) * SUB)
        edge_e = pltpu.roll(cole[rs, :], (2 * LANES - 1) - a, 1)
        edge_w = pltpu.roll(-colw[rs, :], LANES - a, 1)
        flows[-1] = jnp.where(lane == LANES - 1, edge_e, flows[-1])
        for j in range(n_j):
            at = tile(i, j)
            came = jnp.where(lane == 0, backs[j - 1] if j else edge_w, backs[j])
            moved = adj[j] - (out[j] + flows[j] - came)
            fish = fish_ref[at]
            survive = jnp.exp2(death - gear2 * fish)
            caught = catch[i * SUB // BY, j, pl.ds(a, 1), :]
            value = survive * moved + fish * caught
            if recruit is not None:
                value = value + recruit[at] * mat
            out_ref[(k,) + at] = value
            if lines is not None and i == 0:
                lines[0][j, pl.ds(a, 1), :] = value[0:1]
            if lines is not None and i == n_i - 1:
                lines[1][j, pl.ds(a, 1), :] = value[SUB - 1 : SUB]
        now = after


def read_plane(ref, k, ys, xs):
    if ref.dtype == f32:
        return ref[k, ys, xs]
    low = ys.start // 16 * 16
    wide = ref[k, low : low + 16, xs].astype(f32)
    return wide[ys.start - low : ys.stop - low]


def all_cohorts(c, step, count, par_ref, later_ref, next_ref, recruit_ref, go):
    def loader(a):
        def load(ys, xs):
            value = read_plane(later_ref, a + 1, ys, xs)
            if recruit_ref is not None:
                value = value + recruit_ref[ys, xs] * par_ref[MAT, a + 1]
            return value

        return load

    def body(h, carry):
        for k in range(PAIR):
            go(h * PAIR + k, step * count + h * PAIR + k, loader(step * count + h * PAIR + k))
        return carry

    final = step == c.ages // count - 1
    turns = count // PAIR
    lax.fori_loop(0, jnp.where(final, turns - 1, turns) if c.ages > count else turns - 1, body, 0)

    def rest():
        for k in range(count - PAIR, count):
            a = c.ages - count + k
            go(k, a, loader(a) if a + 1 < c.ages else lambda ys, xs: next_ref[ys, xs])

    if c.ages > count:
        pl.when(final)(rest)
    else:
        rest()


def first_kernel(c, *refs):
    refs = list(refs)

    def take(n):
        out = refs[:n]
        del refs[:n]
        return out

    pos_ref, par_ref, parv_ref, later_ref = take(4)
    own, got = take(4), take(4)
    sea_ref, prey_ref, heat_ref, fish_ref = take(4)
    fleet_refs = take(c.n_fleet)
    plane_out, openv, openh, forage, heat4, rowc, colw, cole, catch = take(9)
    rows, cols, ages, months = c.rows, c.cols, c.ages, c.months
    blocks_y, blocks_x = rows // BY, cols // BX
    sea = sea_ref[...].astype(f32)
    line = lax.broadcasted_iota(jnp.int32, (rows, cols), 0)
    column = lax.broadcasted_iota(jnp.int32, (rows, cols), 1)
    openv[...] = jnp.where(line == rows - 1, 0.0, sea * pltpu.roll(sea, rows - 1, 0))
    openh[...] = jnp.where(column == cols - 1, 0.0, sea * pltpu.roll(sea, cols - 1, 1))
    for t in range(months):
        heat4[t] = heat_ref[t] * 0.25
        forage[t] = sea * prey_ref[t]
    edge_flux(c, pos_ref, parv_ref, sea_ref, forage.at[c.month], heat4.at[c.month], own, got, got, rowc, colw, cole)

    flat = []
    for ref in fleet_refs:
        flat += [ref[:, 0:LANES], ref[:, LANES : 2 * LANES]]
    flat = jnp.concatenate(flat, axis=0)
    names = flat[:, months * ages : months * ages + 1]
    turned = flat.T[0 : months * ages]
    base = ((pos_ref[1] * c.sizes[2] + pos_ref[2]) * (blocks_y * blocks_x)).astype(f32)
    block_col = (lax.broadcasted_iota(jnp.int32, (flat.shape[0], cols), 1) // BX).astype(f32)
    gear = column_of(parv_ref, GEAR, ages)
    for by in range(blocks_y):
        named = (block_col == names - (base + by * blocks_x)).astype(f32)
        sums = jnp.dot(turned, named, precision=lax.Precision.HIGHEST, preferred_element_type=f32)
        for t in range(months):
            for j in range(cols // LANES):
                catch[t, by, j] = gear * sums[t * ages : (t + 1) * ages, j * LANES : (j + 1) * LANES]

    tables = (openv, openh, forage.at[c.month], heat4.at[c.month], fish_ref, rowc, colw, cole, catch.at[c.month])
    advance(c, 0, 0, par_ref, lambda ys, xs: read_plane(later_ref, 1, ys, xs), tables, plane_out)
    plane_out[0, rows : rows + SUB, :] = jnp.broadcast_to(
        jnp.broadcast_to(parv_ref[MAT : MAT + 1, 0:1], (1, cols)), (SUB, cols)
    )


def month_kernel(c, *refs):
    refs = list(refs)

    def take(n):
        out = refs[:n]
        del refs[:n]
        return out

    par_ref, later_ref, next_ref, fish_ref = take(4)
    openv, openh, forage, heat4, rowc, colw, cole, catch = take(8)
    out_ref, top_out, bottom_out, west_out, east_out = take(5)
    tables = (openv, openh, forage.at[c.month], heat4.at[c.month], fish_ref, rowc, colw, cole, catch.at[c.month])

    def go(k, a, load):
        advance(c, k, a, par_ref, load, tables, out_ref, lines=(top_out, bottom_out))

    all_cohorts(c, 0, c.ages, par_ref, later_ref, next_ref, None, go)
    lane = lax.broadcasted_iota(jnp.int32, (SUB, LANES), 1)
    for i in range(c.rows // SUB):
        rs = slice(i * SUB, (i + 1) * SUB)
        for dst, lo, by in ((west_out, 0, 0), (east_out, c.cols - LANES, 1)):
            found = jnp.zeros((SUB, LANES), f32)
            for k in range(c.ages):
                value = out_ref[k, rs, lo : lo + LANES]
                found = jnp.where(lane == k, pltpu.roll(value, k + by, 1) if k + by else value, found)
            dst[rs, :] = found


def last_kernel(c, *refs):
    refs = list(refs)

    def take(n):
        out = refs[:n]
        del refs[:n]
        return out

    pos_ref, par_ref, parv_ref, later_ref, next_ref, recruit_ref, sea_ref, fish_ref, yield_ref = take(9)
    openv, openh, forage, heat4, catch = take(5)
    own, got, msgs = take(4), take(4), take(4)
    term_refs = take(c.n_terms)
    bcast_refs = take(c.n_bcast)
    out_ref, grad_ref = take(2)
    rowc, colw, cole, final_recruit = take(4)
    rows, months = c.rows, c.months
    step = pl.program_id(0)

    @pl.when(step == 0)
    def _():
        edge_flux(
            c, pos_ref, parv_ref, sea_ref, forage.at[c.month], heat4.at[c.month], own, got, msgs, rowc, colw, cole
        )
        sea = sea_ref[...].astype(f32)
        totals = [functools.reduce(jnp.add, [r[t] for r in term_refs]) for t in range(months + 1)]
        first = bcast_refs[0][...] * (pos_ref[0] == 0).astype(f32)
        first = first + bcast_refs[1][...] * (pos_ref[0] == c.sizes[0] - 1).astype(f32)
        for ref in bcast_refs[2:]:
            first = first + ref[...]
        first = first[0:rows] + recruit_ref[...] * first[rows : rows + 1]
        ratios = [1.0 / (1.0 + totals[t]) for t in range(months)]
        grad_ref[...] = (totals[months] * totals[1] * ratios[1] + first * totals[0] * ratios[0]) * sea
        final_recruit[...] = first * sea * yield_ref[...] * ratios[0] * ratios[0]

    tables = (openv, openh, forage.at[c.month], heat4.at[c.month], fish_ref, rowc, colw, cole, catch.at[c.month])

    def go(k, a, load):
        advance(c, k, a, par_ref, load, tables, out_ref, recruit=final_recruit)

    all_cohorts(c, step, GROUP, par_ref, later_ref, next_ref, recruit_ref, go)


def cost(planes, rows, cols):
    cells = planes * rows * cols
    return pl.CostEstimate(flops=60 * cells, bytes_accessed=8 * cells, transcendentals=2 * cells)


def edge_shapes(ages, rows, cols):
    return [
        jax.ShapeDtypeStruct((2, cols // LANES, ages, LANES), f32),
        jax.ShapeDtypeStruct((rows, LANES), f32),
        jax.ShapeDtypeStruct((rows, LANES), f32),
    ]


def first_cohort(sizes, pos, par, fin, own, got, sea, prey, heat, fish, fleet_blocks):
    ages, rows, cols = fin.shape
    months = prey.shape[0]
    c = Cfg(rows=rows, cols=cols, ages=ages, months=months, month=months - 1, sizes=sizes, n_fleet=len(fleet_blocks))
    operands = [pos, par, par, fin, *own, *got, sea, prey, heat, fish]
    at = len(operands)
    operands += [block for block, _ in fleet_blocks]

    def kernel(*refs):
        refs = list(refs)
        for k, (block, start) in enumerate(fleet_blocks):
            if start:
                refs[at + k] = refs[at + k].at[start : block.shape[0]]
        first_kernel(c, *refs)

    plane = jax.ShapeDtypeStruct((rows, cols), f32)
    stack = jax.ShapeDtypeStruct((months, rows, cols), f32)
    out_shape = [jax.ShapeDtypeStruct((1, rows + SUB, cols), f32), plane, plane, stack, stack]
    out_shape += edge_shapes(ages, rows, cols)
    out_shape.append(jax.ShapeDtypeStruct((months, rows // BY, cols // LANES, ages, LANES), f32))
    return pl.pallas_call(
        kernel,
        in_specs=[whole(SMEM), whole(SMEM)] + [whole()] * (len(operands) - 2),
        out_specs=[whole()] * len(out_shape),
        out_shape=out_shape,
        cost_estimate=cost(4, rows, cols),
        compiler_params=params_of(8),
        name="first_cohort",
    )(*operands)


def month_step(sizes, par, fin, nxt, fish, fields, edges, catch):
    ages, rows, cols = fin.shape
    months = catch.shape[0]
    c = Cfg(rows=rows, cols=cols, ages=ages, months=months, month=months - 1, sizes=sizes)
    operands = [par, fin, nxt, fish, *fields, *edges, catch]
    line = jax.ShapeDtypeStruct((cols // LANES, ages, LANES), f32)
    column = jax.ShapeDtypeStruct((rows, LANES), f32)
    return pl.pallas_call(
        functools.partial(month_kernel, c),
        in_specs=[whole(SMEM)] + [whole()] * (len(operands) - 1),
        out_specs=[whole()] * 5,
        out_shape=[jax.ShapeDtypeStruct((ages, rows, cols), f32), line, line, column, column],
        cost_estimate=cost(ages, rows, cols),
        compiler_params=params_of(16),
        name="month_step",
    )(*operands)


def month_last(sizes, pos, par, later, nxt, recruit, sea, fish, yields, fields, catch, own, got, msgs, terms, bcasts):
    ages, rows, cols = later.shape
    months = catch.shape[0]
    c = Cfg(
        rows=rows, cols=cols, ages=ages, months=months, month=0, sizes=sizes, n_terms=len(terms), n_bcast=len(bcasts)
    )
    operands = [pos, par, par, later, nxt, recruit, sea, fish, yields, *fields, catch, *own, *got, *msgs]
    operands += [*terms, *bcasts]
    scratch = [pltpu.VMEM(x.shape, f32) for x in edge_shapes(ages, rows, cols)]
    return pl.pallas_call(
        functools.partial(last_kernel, c),
        grid=(ages // GROUP,),
        in_specs=[whole(SMEM), whole(SMEM)] + [whole()] * (len(operands) - 2),
        out_specs=[pl.BlockSpec((GROUP, rows, cols), lambda i: (i, 0, 0)), whole()],
        out_shape=[jax.ShapeDtypeStruct((ages, rows, cols), f32), jax.ShapeDtypeStruct((rows, cols), f32)],
        scratch_shapes=scratch + [pltpu.VMEM((rows, cols), f32)],
        cost_estimate=cost(ages, rows, cols),
        compiler_params=params_of(16),
        name="month_last",
    )(*operands)


def habitat_of(forage, heat, ideal, tau):
    off = heat - ideal
    return forage * (tau / (1.0 + off * off))


def shards(
    saved,
    fin,
    prey,
    heat,
    sea,
    fish,
    yields,
    death,
    gear,
    kappa,
    tau,
    ideal,
    breeding,
    landing,
    east_piece,
    north_piece,
    patch,
    bounds,
):
    months, ages, rows, cols = saved.shape
    n_coh, n_lat, n_lon = sizes = tuple(lax.axis_size(axis) for axis in ("coh", "lat", "lon"))
    at_coh, at_lat, at_lon = (lax.axis_index(axis) for axis in ("coh", "lat", "lon"))
    pos = jnp.stack([at_coh, at_lat, at_lon]).astype(jnp.int32)
    cohort_age = at_coh * ages + jnp.arange(ages)
    nblocks = (rows // BY) * (cols // BX)
    inside = (cohort_age[None, :] >= bounds[:, 0:1]) & (cohort_age[None, :] < bounds[:, 1:2])
    masked = (landing * inside[:, None, :].astype(f32)).reshape(landing.shape[0], months * ages)
    names = ((north_piece * n_lon + east_piece[:, 0]) * nblocks + patch).astype(f32)
    fleet = jnp.concatenate([masked, names[:, None]], axis=1)
    fleet = jnp.pad(fleet, ((0, 0), (0, LANES - fleet.shape[1])))

    first = fin[0].astype(f32)
    nxt = shift(first, "coh", -1)
    fleet_lon = [fleet] + [shift(fleet, "lon", d) for d in range(1, n_lon)]
    terms = first_terms(spawn_parts(pos, breeding, ages * n_coh, saved, first, first), "coh")

    ahead, back, east, west, both, fleet_pack, later_last, par = pack_edges(
        sizes, pos, fin, nxt, sea, prey, heat, fleet_lon, (death, gear, kappa, tau, ideal, breeding)
    )
    from_west, from_east = swap_edges(east, west, both, "lon")
    from_before, from_after = shift(ahead, "lat", 1), shift(back, "lat", -1)
    start = ahead.shape[0] - fleet_pack.shape[0]
    terms = other_terms(terms, "coh", both)
    fleet_blocks = [(ahead, start), (from_before, start)]
    if n_lat > 2:
        fleet_blocks.append((from_after, start))
    fleet_blocks += [(shift(fleet_pack, "lat", d), 0) for d in range(2, n_lat - 1)]

    own = (ahead, back, east, west)
    msgs = (from_before, from_after, from_west, from_east)
    plane, openv, openh, forage, heat4, *edges, catch = first_cohort(
        sizes, pos, par, fin, own, msgs, sea, prey, heat, fish, fleet_blocks
    )
    plane = plane.reshape(rows + SUB, cols)
    fields = (openv, openh, forage, heat4)
    down = shift(plane, "coh", -1)
    bcasts = [plane, down] + [lax.ppermute(plane, "coh", [(0, j)]) for j in range(1, n_coh - 1)]
    later, *edges = month_step(sizes, par, fin, later_last, fish, fields, edges, catch)
    ahead, back, east, west, both, recruit, nxt = recruit_edges(
        sizes, months - 1, pos, par, sea, yields, down, terms, edges
    )
    own = (ahead, back, east, west)
    got = (shift(ahead, "lat", 1), shift(back, "lat", -1), *swap_edges(east, west, both, "lon"))
    return tuple(
        month_last(
            sizes, pos, par, later, nxt, recruit, sea, fish, yields, fields, catch, own, got, msgs, terms, bcasts
        )
    )


def solution(mesh):
    in_specs = (
        P(None, "coh", "lat", "lon"),
        P("coh", "lat", "lon"),
        P(None, "lat", "lon"),
        P(None, "lat", "lon"),
        P("lat", "lon"),
        P("lat", "lon"),
        P("lat", "lon"),
        P("coh"),
        P("coh"),
        P("coh"),
        P("coh"),
        P("coh"),
        P("coh"),
        P(("lat", "lon"), None, "coh"),
        P(("lat", "lon"), None),
        P(("lat", "lon")),
        P(("lat", "lon")),
        P(("lat", "lon"), None),
    )
    out_specs = (P("coh", "lat", "lon"), P("lat", "lon"))

    return jax.shard_map(shards, mesh=mesh, in_specs=in_specs, out_specs=out_specs, check_vma=False)
```

```python
import functools
import math

import jax
import jax.numpy as jnp
from jax import lax
from jax.experimental import pallas as pl
from jax.experimental.pallas import tpu as pltpu
from jax.sharding import PartitionSpec as P

BY = 16
BX = 32
LANES = 128
SUB = 8
GROUP = 8
PAIR = 2
PARTS = 2
SPAWN_MB = 24

f32 = jnp.float32
VMEM = pltpu.MemorySpace.VMEM
SMEM = pltpu.MemorySpace.SMEM
LOG2E = math.log2(math.e)

DEATH, GEAR2, KAPPA, TAU, IDEAL, MAT, GEAR = range(7)


def up_to(value, step):
    return -(-value // step) * step


def whole(memory=VMEM):
    return pl.BlockSpec(memory_space=memory)


def params_of(limit=48):
    return pltpu.CompilerParams(vmem_limit_bytes=limit * 2**20)


def shift(x, axis, distance):
    n = lax.axis_size(axis)
    return lax.ppermute(x, axis, [(i, (i + distance) % n) for i in range(n)])


def swap_edges(ahead, back, both, axis):
    n = lax.axis_size(axis)
    if n == 1:
        return ahead, back
    if n == 2:
        got = shift(both, axis, 1)
        return got, got
    return shift(ahead, axis, 1), shift(back, axis, -1)


def spawn_kernel(months, ages, total_ages, pos_ref, breed_ref, saved_ref, first_ref, _, out_ref):
    mat = [(pos_ref[0] * ages + (a + 1)).astype(f32) / total_ages * breed_ref[a] for a in range(ages)]
    for t in range(months):
        total = saved_ref[t, 0].astype(f32) * mat[0]
        for a in range(1, ages):
            total = total + saved_ref[t, a].astype(f32) * mat[a]
        out_ref[t] = total
    youngest = (pos_ref[0] == 0).astype(f32)
    out_ref[months] = first_ref[...] * youngest


def spawn_parts(pos, breeding, total_ages, saved, first, ahead_of):
    months, ages, rows, cols = saved.shape
    step = 16
    return pl.pallas_call(
        functools.partial(spawn_kernel, months, ages, total_ages),
        grid=(rows // step,),
        in_specs=[
            whole(SMEM),
            whole(SMEM),
            pl.BlockSpec((months, ages, step, cols), lambda i: (0, 0, i, 0)),
            pl.BlockSpec((step, cols), lambda i: (i, 0)),
            pl.BlockSpec(memory_space=pl.ANY),
        ],
        out_specs=pl.BlockSpec((months + 1, step, cols), lambda i: (0, i, 0)),
        out_shape=jax.ShapeDtypeStruct((months + 1, rows, cols), f32),
        compiler_params=params_of(SPAWN_MB),
        name="spawn_parts",
    )(pos, breeding, saved, first, ahead_of)


def add_kernel(a_ref, b_ref, _, out_ref):
    out_ref[...] = a_ref[...] + b_ref[...]


def add_after(a, b, ahead_of):
    return pl.pallas_call(
        add_kernel,
        in_specs=[whole(), whole(), pl.BlockSpec(memory_space=pl.ANY)],
        out_specs=whole(),
        out_shape=jax.ShapeDtypeStruct(a.shape, a.dtype),
        compiler_params=params_of(8),
        name="add_after",
    )(a, b, ahead_of)


def flipped(x, axis, reach):
    return lax.ppermute(x, axis, [(i, i ^ reach) for i in range(lax.axis_size(axis))])


def first_terms(x, axis):
    n = lax.axis_size(axis)
    if n & (n - 1):
        return [x] + [shift(x, axis, d) for d in range(1, n)]
    return [x, flipped(x, axis, 1)] if n > 1 else [x]


def other_terms(terms, axis, ahead_of):
    n = lax.axis_size(axis)
    if n & (n - 1):
        return terms
    reach = 2
    while reach < n:
        mine = add_after(*terms, ahead_of)
        terms = [mine, flipped(mine, axis, reach)]
        reach *= 2
    return terms


def pack_kernel(months, ages, sizes, fleets, *refs):
    pos_ref, fin_ref, next_ref, sea_ref, prey_ref, heat_ref = refs[:6]
    fleet_refs = refs[6 : 6 + fleets]
    death_ref, gear_ref, kappa_ref, tau_ref, ideal_ref, breed_ref = refs[6 + fleets : 12 + fleets]
    ahead_ref, back_ref, east_ref, west_ref, fleet_out, later_ref, table_ref, openv, openh, forage, heat4 = refs[12 + fleets :]
    n_coh, n_lat, n_lon = sizes
    age = lax.broadcasted_iota(jnp.int32, (1, ages), 1) + (pos_ref[0] * ages + 1)
    table_ref[...] = jnp.zeros_like(table_ref)
    table_ref[DEATH : DEATH + 1, 0:ages] = death_ref[...] * -LOG2E
    table_ref[GEAR2 : GEAR2 + 1, 0:ages] = gear_ref[...] * LOG2E
    table_ref[KAPPA : KAPPA + 1, 0:ages] = kappa_ref[...]
    table_ref[TAU : TAU + 1, 0:ages] = tau_ref[...]
    table_ref[IDEAL : IDEAL + 1, 0:ages] = ideal_ref[...] * 0.25
    table_ref[MAT : MAT + 1, 0:ages] = age.astype(f32) / (ages * n_coh) * breed_ref[...]
    table_ref[GEAR : GEAR + 1, 0:ages] = gear_ref[...]
    rows, cols = next_ref.shape
    keep = (pos_ref[0] < n_coh - 1).astype(f32)
    last = next_ref[...] * keep
    later_ref[...] = last

    count = fleet_refs[0].shape[0]
    half = count * fleets // 2
    for k, ref in enumerate(fleet_refs):
        at = k * count
        if count <= half:
            side, line = divmod(at, half)
            fleet_out[line : line + count, side * LANES : (side + 1) * LANES] = ref[...]
        else:
            fleet_out[0:half, 0:LANES] = ref[0:half, :]
            fleet_out[0:half, LANES : 2 * LANES] = ref[half:, :]

    band = 16
    for a in range(ages):
        if a + 1 < ages:
            top = fin_ref[a + 1, 0:band, :].astype(f32)[0:1]
            bottom = fin_ref[a + 1, rows - band : rows, :].astype(f32)[band - 1 : band]
        else:
            top, bottom = last[0:1], last[rows - 1 : rows]
        back_ref[a : a + 1, :] = top
        ahead_ref[a : a + 1, :] = bottom
    fields = [sea_ref[...].astype(f32)]
    for t in range(months):
        fields += [prey_ref[t], heat_ref[t]]
    for k, field in enumerate(fields):
        back_ref[ages + k : ages + k + 1, :] = field[0:1]
        ahead_ref[ages + k : ages + k + 1, :] = field[rows - 1 : rows]
    blank = jnp.zeros((1, cols), f32)
    start = up_to(ages + len(fields), SUB)
    for k in range(ages + len(fields), start):
        back_ref[k : k + 1, :] = blank
        ahead_ref[k : k + 1, :] = blank
    back_ref[start:, 0 : 2 * LANES] = fleet_out[...]
    ahead_ref[start:, 0 : 2 * LANES] = fleet_out[...]

    lane = lax.broadcasted_iota(jnp.int32, (rows, LANES), 1)
    east = jnp.zeros((rows, LANES), f32)
    west = jnp.zeros((rows, LANES), f32)
    for k in range(ages + len(fields)):
        if k + 1 < ages:
            left = fin_ref[k + 1, :, 0:LANES].astype(f32)
            right = fin_ref[k + 1, :, cols - LANES : cols].astype(f32)
        else:
            plane = last if k + 1 == ages else fields[k - ages]
            left, right = plane[:, 0:LANES], plane[:, cols - LANES : cols]
        west = jnp.where(lane == k, pltpu.roll(left, k, 1) if k else left, west)
        east = jnp.where(lane == k, pltpu.roll(right, k + 1, 1), east)
    east_ref[...] = east
    west_ref[...] = west

    sea = fields[0]
    line = lax.broadcasted_iota(jnp.int32, (rows, cols), 0)
    column = lax.broadcasted_iota(jnp.int32, (rows, cols), 1)
    openv[...] = jnp.where(line == rows - 1, 0.0, sea * pltpu.roll(sea, rows - 1, 0))
    openh[...] = jnp.where(column == cols - 1, 0.0, sea * pltpu.roll(sea, cols - 1, 1))
    for t in range(months):
        heat4[t] = heat_ref[t] * 0.25
        forage[t] = sea * prey_ref[t]


def relay_kernel(side, pos_ref, east_ref, west_ref, _, *refs):
    *block_refs, both_ref, gathered_ref = refs
    rows = east_ref.shape[0]
    at = 0
    for ref in block_refs:
        for half in range(2):
            gathered_ref[at : at + side, :] = ref[ref.shape[0] - side :, half * LANES : (half + 1) * LANES]
            at += side
    both_ref[0:rows, :] = jnp.where(pos_ref[2] == 0, east_ref[...], west_ref[...])
    both_ref[rows:, :] = gathered_ref[...]


def relay(pos, east, west, ahead_of, blocks, side):
    rows = east.shape[0]
    tall = 2 * side * len(blocks)
    return pl.pallas_call(
        functools.partial(relay_kernel, side),
        in_specs=[whole(SMEM), whole(), whole(), pl.BlockSpec(memory_space=pl.ANY)] + [whole()] * len(blocks),
        out_specs=[whole()] * 2,
        out_shape=[jax.ShapeDtypeStruct((rows + tall, LANES), f32), jax.ShapeDtypeStruct((tall, LANES), f32)],
        compiler_params=params_of(8),
        name="relay",
    )(pos, east, west, ahead_of, *blocks)


def pack_edges(sizes, pos, fin, nxt, sea, prey, heat, fleet_blocks, rates):
    ages, rows, cols = fin.shape
    months = prey.shape[0]
    half = len(fleet_blocks) * fleet_blocks[0].shape[0] // 2
    tall = up_to(ages + 1 + 2 * months, SUB) + half
    line = jax.ShapeDtypeStruct((tall, cols), f32)
    column = jax.ShapeDtypeStruct((rows, LANES), f32)
    return pl.pallas_call(
        functools.partial(pack_kernel, months, ages, sizes, len(fleet_blocks)),
        in_specs=[whole(SMEM)] + [whole()] * (5 + len(fleet_blocks) + len(rates)),
        out_specs=[whole()] * 11,
        out_shape=[
            line,
            line,
            column,
            column,
            jax.ShapeDtypeStruct((half, 2 * LANES), f32),
            jax.ShapeDtypeStruct((rows, cols), f32),
            jax.ShapeDtypeStruct((SUB, LANES), f32),
            jax.ShapeDtypeStruct((rows, cols), f32),
            jax.ShapeDtypeStruct((rows, cols), f32),
            jax.ShapeDtypeStruct((months, rows, cols), f32),
            jax.ShapeDtypeStruct((months, rows, cols), f32),
        ],
        compiler_params=params_of(16),
        name="pack_edges",
    )(pos, fin, nxt, sea, prey, heat, *fleet_blocks, *[rate.reshape(1, ages) for rate in rates])


def recruit_kernel(c, terms, *refs):
    pos_ref, par_ref, parv_ref, sea_ref, yield_ref, fish_ref, nxt_ref = refs[:7]
    term_refs = refs[7 : 7 + terms]
    rowc, colw, cole, catch, _ = refs[7 + terms : 12 + terms]
    all_ref, ahead_out, back_out, east_out, west_out, both_out, recruit_out, last_out, top, bottom = refs[12 + terms :]
    rows, cols, ages, months = c.rows, c.cols, c.ages, c.months
    n_i, n_j = rows // SUB, cols // LANES
    keep = (pos_ref[0] < c.sizes[0] - 1).astype(f32)
    spawning = functools.reduce(jnp.add, [r[c.month] for r in term_refs])
    first = functools.reduce(jnp.add, [r[months] for r in term_refs])
    ratio = 1.0 / (1.0 + spawning)
    recruit_out[...] = first * sea_ref[...].astype(f32) * yield_ref[...] * ratio * ratio
    last = (nxt_ref[0:rows, :] + recruit_out[...] * nxt_ref[rows : rows + 1, :]) * keep
    last_out[...] = last

    def body(h, carry):
        for k in range(PAIR):
            a = h * PAIR + k
            mat = par_ref[MAT, a]
            for i in range(n_i):
                for j in range(n_j):
                    ys, xs = slice(i * SUB, (i + 1) * SUB), slice(j * LANES, (j + 1) * LANES)
                    value = at_edges(
                        c, i, j, a, all_ref[a, ys, xs], fish_ref, rowc, colw, cole, catch.at[c.month]
                    )
                    value = value + recruit_out[ys, xs] * mat
                    all_ref[a, ys, xs] = value
                    if i == 0:
                        top[j, pl.ds(a, 1), :] = value[0:1]
                    if i == n_i - 1:
                        bottom[j, pl.ds(a, 1), :] = value[SUB - 1 : SUB]
        return carry

    lax.fori_loop(0, ages // PAIR, body, 0)
    place = lax.broadcasted_iota(jnp.int32, (ages, cols), 0)
    for src, dst, row in ((top, back_out, 0), (bottom, ahead_out, rows - 1)):
        full = jnp.concatenate([src[j] for j in range(n_j)], axis=1)
        dst[...] = jnp.where(place == ages - 1, last[row : row + 1, :], pltpu.roll(full, ages - 1, 0))
    lane = lax.broadcasted_iota(jnp.int32, (SUB, LANES), 1)
    for i in range(n_i):
        rs = slice(i * SUB, (i + 1) * SUB)
        for dst, lo, by, col in ((west_out, 0, 0, 0), (east_out, cols - LANES, 1, cols - 1)):
            found = jnp.where(lane == ages - 1, last_out[rs, col : col + 1], 0.0)
            for k in range(1, ages):
                value = all_ref[k, rs, lo : lo + LANES]
                found = jnp.where(lane == k - 1, pltpu.roll(value, k - 1 + by, 1) if k - 1 + by else value, found)
            dst[rs, :] = found
    both_out[...] = jnp.where(pos_ref[2] == 0, east_out[...], west_out[...])


def recruit_edges(sizes, pos, par, sea, yields, fish, nxt, terms, edges, catch, inner):
    ages, rows, cols = inner.shape
    months = terms[0].shape[0] - 1
    c = Cfg(rows=rows, cols=cols, ages=ages, months=months, month=months - 1, sizes=sizes)
    line = jax.ShapeDtypeStruct((ages, cols), f32)
    column = jax.ShapeDtypeStruct((rows, LANES), f32)
    operands = [pos, par, par, sea, yields, fish, nxt, *terms, *edges, catch, inner]
    return pl.pallas_call(
        functools.partial(recruit_kernel, c, len(terms)),
        in_specs=[whole(SMEM), whole(SMEM)] + [whole()] * (len(operands) - 2),
        out_specs=[whole()] * 8,
        out_shape=[jax.ShapeDtypeStruct(inner.shape, f32), line, line, column, column, column]
        + [jax.ShapeDtypeStruct((rows, cols), f32)] * 2,
        scratch_shapes=[pltpu.VMEM((cols // LANES, ages, LANES), f32)] * 2,
        input_output_aliases={len(operands) - 1: 0},
        cost_estimate=pl.CostEstimate(flops=16 * inner.size, bytes_accessed=8 * inner.size, transcendentals=0),
        compiler_params=params_of(8),
        name="recruit_edges",
    )(*operands)


class Cfg:
    def __init__(self, **kw):
        self.__dict__.update(kw)


def column_of(par_ref, k, ages):
    down = lax.broadcasted_iota(jnp.int32, (ages, LANES), 0)
    across = lax.broadcasted_iota(jnp.int32, (ages, LANES), 1)
    row = jnp.broadcast_to(par_ref[k : k + 1, :], (ages, LANES))
    return jnp.sum(jnp.where(down == across, row, 0.0), axis=1, keepdims=True)


def edge_flux(c, pos_ref, parv_ref, sea_ref, forage_ref, heat4_ref, own, got, msgs, rowc, colw, cole, fish_ref=None):
    rows, cols, ages = c.rows, c.cols, c.ages
    n_coh, n_lat, n_lon = c.sizes
    own_ahead, own_back, own_east, own_west = own
    from_before, from_after, from_west, from_east = got
    msg_before, msg_after, msg_west, msg_east = msgs
    sea_line, prey_line, heat_line = ages, ages + 1 + 2 * c.month, ages + 2 + 2 * c.month
    kappa, tau, ideal, death, gear2 = (column_of(parv_ref, k, ages) for k in (KAPPA, TAU, IDEAL, DEATH, GEAR2))
    has = [
        (pos_ref[1] > 0).astype(f32),
        (pos_ref[1] < n_lat - 1).astype(f32),
        (pos_ref[2] > 0).astype(f32),
        (pos_ref[2] < n_lon - 1).astype(f32),
    ]
    for k, (row, own, got, msg) in enumerate(
        ((0, own_back, from_before, msg_before), (rows - 1, own_ahead, from_after, msg_after))
    ):
        here = habitat_of(forage_ref[row : row + 1, :], heat4_ref[row : row + 1, :], ideal, tau)
        sea_there = msg[sea_line : sea_line + 1, :]
        there = habitat_of(
            sea_there * msg[prey_line : prey_line + 1, :], msg[heat_line : heat_line + 1, :] * 0.25, ideal, tau
        )
        both = sea_ref[row : row + 1, :].astype(f32) * sea_there * has[k]
        flux = both * (kappa + jnp.maximum(there - here, 0.0)) * (own[0:ages, :] - got[0:ages, :])
        if fish_ref is not None:
            flux = flux * jnp.exp2(death - gear2 * fish_ref[row : row + 1, :])
        for j in range(cols // LANES):
            rowc[k, j] = flux[:, j * LANES : (j + 1) * LANES]
    kappa, tau, ideal, death, gear2 = (parv_ref[k : k + 1, :] for k in (KAPPA, TAU, IDEAL, DEATH, GEAR2))
    for k, (col, own, got, msg, dst) in enumerate(
        ((0, own_west, from_west, msg_west, colw), (cols - 1, own_east, from_east, msg_east, cole))
    ):
        here = habitat_of(forage_ref[:, col : col + 1], heat4_ref[:, col : col + 1], ideal, tau)
        msg = msg.at[0:rows]
        sea_there = msg[:, sea_line : sea_line + 1]
        there = habitat_of(
            sea_there * msg[:, prey_line : prey_line + 1], msg[:, heat_line : heat_line + 1] * 0.25, ideal, tau
        )
        both = sea_ref[:, col : col + 1].astype(f32) * sea_there * has[2 + k]
        flux = both * (kappa + jnp.maximum(there - here, 0.0)) * (own[0:rows, :] - got[0:rows, :])
        if fish_ref is not None:
            flux = flux * jnp.exp2(death - gear2 * fish_ref[:, col : col + 1])
        dst[...] = flux


def advance(c, k, a, par_ref, load, tables, out_ref, recruit=None):
    openv, openh, forage, heat4, fish_ref, *edges = tables
    if edges:
        rowc, colw, cole, catch = edges
    n_i, n_j = c.rows // SUB, c.cols // LANES
    lane = lax.broadcasted_iota(jnp.int32, (SUB, LANES), 1)
    sub = lax.broadcasted_iota(jnp.int32, (SUB, LANES), 0)
    kappa, tau, ideal = par_ref[KAPPA, a], par_ref[TAU, a], par_ref[IDEAL, a]
    death, gear2 = par_ref[DEATH, a], par_ref[GEAR2, a]
    if recruit is not None:
        mat = par_ref[MAT, a]

    def tile(i, j):
        return slice(i * SUB, (i + 1) * SUB), slice(j * LANES, (j + 1) * LANES)

    def strip(i):
        adj, hab = [], []
        for j in range(n_j):
            at = tile(i, j)
            adj.append(load(*at))
            off = heat4[at] - ideal
            hab.append(forage[at] * tau * pl.reciprocal(1.0 + off * off, approx=False))
        return adj, hab, [pltpu.roll(v, SUB - 1, 0) for v in adj], [pltpu.roll(v, SUB - 1, 0) for v in hab]

    now = strip(0)
    above = [jnp.zeros((SUB, LANES), f32)] * n_j
    if edges:
        above = [jnp.broadcast_to(-rowc[0, j, pl.ds(a, 1), :], (SUB, LANES)) for j in range(n_j)]
        below = [jnp.broadcast_to(rowc[1, j, pl.ds(a, 1), :], (SUB, LANES)) for j in range(n_j)]
    for i in range(n_i):
        after = strip(i + 1) if i + 1 < n_i else now
        adj, hab, adj_up, hab_up = now
        out = [None] * n_j
        for j in range(n_j):
            at = tile(i, j)
            adj_d = jnp.where(sub == SUB - 1, after[2][j], adj_up[j])
            hab_d = jnp.where(sub == SUB - 1, after[3][j], hab_up[j])
            g = hab_d - hab[j]
            d = openv[at] * (adj[j] - adj_d)
            p = jnp.maximum(g, 0.0) + kappa
            f = p * d
            if edges and i == n_i - 1:
                f = jnp.where(sub == SUB - 1, below[j], f)
            turned = pltpu.roll((p - g) * d, 1, 0)
            out[j] = f - jnp.where(sub == 0, above[j], turned)
            above[j] = turned
        adj_l = [pltpu.roll(v, LANES - 1, 1) for v in adj]
        hab_l = [pltpu.roll(v, LANES - 1, 1) for v in hab]
        flows, backs = [], []
        for j in range(n_j):
            at = tile(i, j)
            if j + 1 < n_j:
                adj_d = jnp.where(lane == LANES - 1, adj_l[j + 1], adj_l[j])
                hab_d = jnp.where(lane == LANES - 1, hab_l[j + 1], hab_l[j])
            else:
                adj_d, hab_d = adj_l[j], hab_l[j]
            g = hab_d - hab[j]
            d = openh[at] * (adj[j] - adj_d)
            p = jnp.maximum(g, 0.0) + kappa
            flows.append(p * d)
            backs.append(pltpu.roll((p - g) * d, 1, 1))
        rs = slice(i * SUB, (i + 1) * SUB)
        if edges:
            edge_e = pltpu.roll(cole[rs, :], (2 * LANES - 1) - a, 1)
            edge_w = pltpu.roll(-colw[rs, :], LANES - a, 1)
            flows[-1] = jnp.where(lane == LANES - 1, edge_e, flows[-1])
        else:
            edge_w = jnp.zeros((SUB, LANES), f32)
        for j in range(n_j):
            at = tile(i, j)
            came = jnp.where(lane == 0, backs[j - 1] if j else edge_w, backs[j])
            moved = adj[j] - (out[j] + flows[j] - came)
            fish = fish_ref[at]
            survive = jnp.exp2(death - gear2 * fish)
            value = survive * moved
            if edges:
                value = value + fish * catch[i * SUB // BY, j, pl.ds(a, 1), :]
            if recruit is not None:
                value = value + recruit[at] * mat
            out_ref[(k,) + at] = value
        now = after


def at_edges(c, i, j, a, value, fish_ref, rowc, colw, cole, catch):
    lane = lax.broadcasted_iota(jnp.int32, (SUB, LANES), 1)
    sub = lax.broadcasted_iota(jnp.int32, (SUB, LANES), 0)
    rs = slice(i * SUB, (i + 1) * SUB)
    n_i, n_j = c.rows // SUB, c.cols // LANES
    value = value + fish_ref[rs, j * LANES : (j + 1) * LANES] * catch[i * SUB // BY, j, pl.ds(a, 1), :]
    if i == 0:
        value = value - jnp.where(sub == 0, rowc[0, j, pl.ds(a, 1), :], 0.0)
    if i == n_i - 1:
        value = value - jnp.where(sub == SUB - 1, rowc[1, j, pl.ds(a, 1), :], 0.0)
    if j == 0:
        value = value - jnp.where(lane == 0, pltpu.roll(colw[rs, :], LANES - a, 1), 0.0)
    if j == n_j - 1:
        value = value - jnp.where(lane == LANES - 1, pltpu.roll(cole[rs, :], (2 * LANES - 1) - a, 1), 0.0)
    return value


def read_plane(ref, k, ys, xs):
    if ref.dtype == f32:
        return ref[k, ys, xs]
    low = ys.start // 16 * 16
    wide = ref[k, low : low + 16, xs].astype(f32)
    return wide[ys.start - low : ys.stop - low]


def all_cohorts(c, step, count, par_ref, later_ref, next_ref, recruit_ref, go):
    def loader(a):
        def load(ys, xs):
            value = read_plane(later_ref, a + 1, ys, xs)
            if recruit_ref is not None:
                value = value + recruit_ref[ys, xs] * par_ref[MAT, a + 1]
            return value

        return load

    def body(h, carry):
        for k in range(PAIR):
            go(h * PAIR + k, step * count + h * PAIR + k, loader(step * count + h * PAIR + k))
        return carry

    final = step == c.ages // count - 1
    turns = count // PAIR
    fixed = isinstance(step, int)
    if fixed:
        lax.fori_loop(0, turns - 1 if final else turns, body, 0)
    else:
        lax.fori_loop(0, jnp.where(final, turns - 1, turns), body, 0)

    def rest():
        for k in range(count - PAIR, count):
            a = c.ages - count + k
            go(k, a, loader(a) if a + 1 < c.ages else lambda ys, xs: next_ref[ys, xs])

    if not fixed:
        pl.when(final)(rest)
    elif final:
        rest()


def first_kernel(c, *refs):
    refs = list(refs)

    def take(n):
        out = refs[:n]
        del refs[:n]
        return out

    pos_ref, parv_ref, inner_ref = take(3)
    own, got = take(4), take(4)
    sea_ref, fish_ref = take(2)
    fleet_refs = take(c.n_fleet)
    forage, heat4 = take(2)
    plane_out, rowc, colw, cole, catch = take(5)
    rows, cols, ages, months = c.rows, c.cols, c.ages, c.months
    blocks_y, blocks_x = rows // BY, cols // BX
    edge_flux(c, pos_ref, parv_ref, sea_ref, forage.at[c.month], heat4.at[c.month], own, got, got, rowc, colw, cole, fish_ref)

    flat = jnp.concatenate([ref[...] for ref in fleet_refs], axis=0)
    names = flat[:, months * ages : months * ages + 1]
    turned = flat.T[0 : months * ages]
    base = ((pos_ref[1] * c.sizes[2] + pos_ref[2]) * (blocks_y * blocks_x)).astype(f32)
    block_col = (lax.broadcasted_iota(jnp.int32, (flat.shape[0], cols), 1) // BX).astype(f32)
    gear = column_of(parv_ref, GEAR, ages)
    for by in range(blocks_y):
        named = (block_col == names - (base + by * blocks_x)).astype(f32)
        sums = jnp.dot(turned, named, precision=lax.Precision.HIGHEST, preferred_element_type=f32)
        for t in range(months):
            for j in range(cols // LANES):
                catch[t, by, j] = gear * sums[t * ages : (t + 1) * ages, j * LANES : (j + 1) * LANES]

    for i in range(rows // SUB):
        for j in range(cols // LANES):
            ys, xs = slice(i * SUB, (i + 1) * SUB), slice(j * LANES, (j + 1) * LANES)
            plane_out[0, ys, xs] = at_edges(
                c, i, j, 0, inner_ref[0, ys, xs], fish_ref, rowc, colw, cole, catch.at[c.month]
            )
    plane_out[0, rows : rows + SUB, :] = jnp.broadcast_to(
        jnp.broadcast_to(parv_ref[MAT : MAT + 1, 0:1], (1, cols)), (SUB, cols)
    )


def month_kernel(c, *refs):
    par_ref, later_ref, next_ref, fish_ref, openv, openh, forage, heat4 = refs[:8]
    out_ref = refs[-1]
    tables = (openv, openh, forage.at[c.month], heat4.at[c.month], fish_ref)

    def go(k, a, load):
        advance(c, a, a, par_ref, load, tables, out_ref)

    all_cohorts(c, c.part, c.ages // PARTS, par_ref, later_ref, next_ref, None, go)


def last_kernel(c, *refs):
    refs = list(refs)

    def take(n):
        out = refs[:n]
        del refs[:n]
        return out

    pos_ref, par_ref, parv_ref, later_ref, next_ref, recruit_ref, sea_ref, fish_ref, yield_ref = take(9)
    openv, openh, forage, heat4, catch = take(5)
    own, got, msgs = take(4), take(4), take(4)
    term_refs = take(c.n_terms)
    bcast_refs = take(c.n_bcast)
    out_ref, grad_ref = take(2)
    rowc, colw, cole, final_recruit = take(4)
    rows, months = c.rows, c.months
    step = pl.program_id(0)

    @pl.when(step == 0)
    def _():
        edge_flux(
            c, pos_ref, parv_ref, sea_ref, forage.at[c.month], heat4.at[c.month], own, got, msgs, rowc, colw, cole
        )
        sea = sea_ref[...].astype(f32)
        totals = [functools.reduce(jnp.add, [r[t] for r in term_refs]) for t in range(months + 1)]
        first = bcast_refs[0][...] * (pos_ref[0] == 0).astype(f32)
        first = first + bcast_refs[1][...] * (pos_ref[0] == c.sizes[0] - 1).astype(f32)
        for ref in bcast_refs[2:]:
            first = first + ref[...]
        first = first[0:rows] + recruit_ref[...] * first[rows : rows + 1]
        ratios = [1.0 / (1.0 + totals[t]) for t in range(months)]
        grad_ref[...] = (totals[months] * totals[1] * ratios[1] + first * totals[0] * ratios[0]) * sea
        final_recruit[...] = first * sea * yield_ref[...] * ratios[0] * ratios[0]

    tables = (openv, openh, forage.at[c.month], heat4.at[c.month], fish_ref, rowc, colw, cole, catch.at[c.month])

    def go(k, a, load):
        advance(c, k, a, par_ref, load, tables, out_ref, recruit=final_recruit)

    all_cohorts(c, step, GROUP, par_ref, later_ref, next_ref, None, go)


def cost(planes, rows, cols):
    cells = planes * rows * cols
    return pl.CostEstimate(flops=60 * cells, bytes_accessed=8 * cells, transcendentals=2 * cells)


def edge_shapes(ages, rows, cols):
    return [
        jax.ShapeDtypeStruct((2, cols // LANES, ages, LANES), f32),
        jax.ShapeDtypeStruct((rows, LANES), f32),
        jax.ShapeDtypeStruct((rows, LANES), f32),
    ]


def first_cohort(sizes, pos, par, inner, own, got, sea, fish, fleet_blocks, forage, heat4):
    ages, rows, cols = inner.shape
    months = forage.shape[0]
    c = Cfg(rows=rows, cols=cols, ages=ages, months=months, month=months - 1, sizes=sizes, n_fleet=len(fleet_blocks))
    operands = [pos, par, inner, *own, *got, sea, fish]
    at = len(operands)
    operands += [block for block, _ in fleet_blocks] + [forage, heat4]

    def kernel(*refs):
        refs = list(refs)
        for k, (block, start) in enumerate(fleet_blocks):
            if start:
                refs[at + k] = refs[at + k].at[start : block.shape[0]]
        first_kernel(c, *refs)

    out_shape = [jax.ShapeDtypeStruct((1, rows + SUB, cols), f32)]
    out_shape += edge_shapes(ages, rows, cols)
    out_shape.append(jax.ShapeDtypeStruct((months, rows // BY, cols // LANES, ages, LANES), f32))
    return pl.pallas_call(
        kernel,
        in_specs=[whole(SMEM)] + [whole()] * (len(operands) - 1),
        out_specs=[whole()] * len(out_shape),
        out_shape=out_shape,
        cost_estimate=cost(4, rows, cols),
        compiler_params=params_of(8),
        name="first_cohort",
    )(*operands)


def month_inner(sizes, part, par, fin, nxt, fish, fields, before, ahead_of):
    ages, rows, cols = fin.shape
    months = fields[2].shape[0]
    c = Cfg(rows=rows, cols=cols, ages=ages, months=months, month=months - 1, sizes=sizes, part=part)
    operands = [par, fin, nxt, fish, *fields, ahead_of]
    specs = [whole(SMEM)] + [whole()] * (len(operands) - 2) + [pl.BlockSpec(memory_space=pl.ANY)]
    alias = {}
    if before is not None:
        alias = {len(operands): 0}
        operands.append(before)
        specs.append(whole())
    return pl.pallas_call(
        functools.partial(month_kernel, c),
        in_specs=specs,
        out_specs=whole(),
        out_shape=jax.ShapeDtypeStruct((ages, rows, cols), f32),
        input_output_aliases=alias,
        cost_estimate=cost(ages // PARTS, rows, cols),
        compiler_params=params_of(16),
        name="month_inner",
    )(*operands)


def month_last(sizes, pos, par, later, nxt, recruit, sea, fish, yields, fields, catch, own, got, msgs, terms, bcasts):
    ages, rows, cols = later.shape
    months = catch.shape[0]
    c = Cfg(
        rows=rows, cols=cols, ages=ages, months=months, month=0, sizes=sizes, n_terms=len(terms), n_bcast=len(bcasts)
    )
    operands = [pos, par, par, later, nxt, recruit, sea, fish, yields, *fields, catch, *own, *got, *msgs]
    operands += [*terms, *bcasts]
    scratch = [pltpu.VMEM(x.shape, f32) for x in edge_shapes(ages, rows, cols)]
    return pl.pallas_call(
        functools.partial(last_kernel, c),
        grid=(ages // GROUP,),
        in_specs=[whole(SMEM), whole(SMEM)] + [whole()] * (len(operands) - 2),
        out_specs=[pl.BlockSpec((GROUP, rows, cols), lambda i: (i, 0, 0)), whole()],
        out_shape=[jax.ShapeDtypeStruct((ages, rows, cols), f32), jax.ShapeDtypeStruct((rows, cols), f32)],
        scratch_shapes=scratch + [pltpu.VMEM((rows, cols), f32)],
        cost_estimate=cost(ages, rows, cols),
        compiler_params=params_of(16),
        name="month_last",
    )(*operands)


def habitat_of(forage, heat, ideal, tau):
    off = heat - ideal
    return forage * (tau / (1.0 + off * off))


def shards(
    saved,
    fin,
    prey,
    heat,
    sea,
    fish,
    yields,
    death,
    gear,
    kappa,
    tau,
    ideal,
    breeding,
    landing,
    east_piece,
    north_piece,
    patch,
    bounds,
):
    months, ages, rows, cols = saved.shape
    n_coh, n_lat, n_lon = sizes = tuple(lax.axis_size(axis) for axis in ("coh", "lat", "lon"))
    at_coh, at_lat, at_lon = (lax.axis_index(axis) for axis in ("coh", "lat", "lon"))
    pos = jnp.stack([at_coh, at_lat, at_lon]).astype(jnp.int32)
    cohort_age = at_coh * ages + jnp.arange(ages)
    nblocks = (rows // BY) * (cols // BX)
    inside = (cohort_age[None, :] >= bounds[:, 0:1]) & (cohort_age[None, :] < bounds[:, 1:2])
    masked = (landing * inside[:, None, :].astype(f32)).reshape(landing.shape[0], months * ages)
    names = ((north_piece * n_lon + east_piece[:, 0]) * nblocks + patch).astype(f32)
    fleet = jnp.concatenate([masked, names[:, None]], axis=1)
    fleet = jnp.pad(fleet, ((0, 0), (0, LANES - fleet.shape[1])))

    first = fin[0].astype(f32)
    nxt = shift(first, "coh", -1)
    terms = first_terms(spawn_parts(pos, breeding, ages * n_coh, saved, first, first), "coh")

    ahead, back, east, west, fleet_pack, later_last, par, *fields = pack_edges(
        sizes, pos, fin, nxt, sea, prey, heat, [fleet], (death, gear, kappa, tau, ideal, breeding)
    )
    from_before, from_after = shift(ahead, "lat", 1), shift(back, "lat", -1)
    blocks = [ahead, from_before] + ([from_after] if n_lat > 2 else [])
    blocks += [shift(fleet_pack, "lat", d) for d in range(2, n_lat - 1)]
    inner = month_inner(sizes, 0, par, fin, later_last, fish, fields, None, ahead)
    both, gathered = relay(pos, east, west, inner, blocks, fleet_pack.shape[0])
    terms = other_terms(terms, "coh", both)
    inner = month_inner(sizes, 1, par, fin, later_last, fish, fields, inner, both)
    from_west, from_east = swap_edges(east, west, both, "lon")
    fleet_blocks = [(gathered, 0)]
    if n_lon == 2:
        fleet_blocks.append((from_west, rows))
    else:
        fleet_blocks += [(shift(gathered, "lon", d), 0) for d in range(1, n_lon)]
    own = (ahead, back, east, west)
    msgs = (from_before, from_after, from_west, from_east)
    plane, *edges, catch = first_cohort(
        sizes, pos, par, inner, own, msgs, sea, fish, fleet_blocks, fields[2], fields[3]
    )
    plane = plane.reshape(rows + SUB, cols)
    down = shift(plane, "coh", -1)
    bcasts = [plane, down] + [lax.ppermute(plane, "coh", [(0, j)]) for j in range(1, n_coh - 1)]
    later, ahead, back, east, west, both, recruit, nxt = recruit_edges(
        sizes, pos, par, sea, yields, fish, down, terms, edges, catch, inner
    )
    own = (ahead, back, east, west)
    got = (shift(ahead, "lat", 1), shift(back, "lat", -1), *swap_edges(east, west, both, "lon"))
    return tuple(
        month_last(
            sizes, pos, par, later, nxt, recruit, sea, fish, yields, fields, catch, own, got, msgs, terms, bcasts
        )
    )


def solution(mesh):
    in_specs = (
        P(None, "coh", "lat", "lon"),
        P("coh", "lat", "lon"),
        P(None, "lat", "lon"),
        P(None, "lat", "lon"),
        P("lat", "lon"),
        P("lat", "lon"),
        P("lat", "lon"),
        P("coh"),
        P("coh"),
        P("coh"),
        P("coh"),
        P("coh"),
        P("coh"),
        P(("lat", "lon"), None, "coh"),
        P(("lat", "lon"), None),
        P(("lat", "lon")),
        P(("lat", "lon")),
        P(("lat", "lon"), None),
    )
    out_specs = (P("coh", "lat", "lon"), P("lat", "lon"))

    return jax.shard_map(shards, mesh=mesh, in_specs=in_specs, out_specs=out_specs, check_vma=False)
```

```python
import functools
import math

import jax
import jax.numpy as jnp
from jax import lax
from jax.experimental import pallas as pl
from jax.experimental.pallas import tpu as pltpu
from jax.sharding import PartitionSpec as P

BY = 16
BX = 32
LANES = 128
SUB = 8
GROUP = 8
PAIR = 2
PARTS = 2
BATCH = 8
SPAWN_MB = 24

f32 = jnp.float32
VMEM = pltpu.MemorySpace.VMEM
SMEM = pltpu.MemorySpace.SMEM
LOG2E = math.log2(math.e)

DEATH, GEAR2, KAPPA, TAU, IDEAL, MAT, GEAR = range(7)


def up_to(value, step):
    return -(-value // step) * step


def whole(memory=VMEM):
    return pl.BlockSpec(memory_space=memory)


def params_of(limit=48):
    return pltpu.CompilerParams(vmem_limit_bytes=limit * 2**20)


def shift(x, axis, distance):
    n = lax.axis_size(axis)
    return lax.ppermute(x, axis, [(i, (i + distance) % n) for i in range(n)])


def swap_edges(ahead, back, both, axis):
    n = lax.axis_size(axis)
    if n == 1:
        return ahead, back
    if n == 2:
        got = shift(both, axis, 1)
        return got, got
    return shift(ahead, axis, 1), shift(back, axis, -1)


def spawn_kernel(months, ages, total_ages, pos_ref, breed_ref, saved_ref, first_ref, _, out_ref):
    mat = [(pos_ref[0] * ages + (a + 1)).astype(f32) / total_ages * breed_ref[a] for a in range(ages)]
    for t in range(months):
        total = saved_ref[t, 0].astype(f32) * mat[0]
        for a in range(1, ages):
            total = total + saved_ref[t, a].astype(f32) * mat[a]
        out_ref[t] = total
    youngest = (pos_ref[0] == 0).astype(f32)
    out_ref[months] = first_ref[...] * youngest


def spawn_parts(pos, breeding, total_ages, saved, first, ahead_of):
    months, ages, rows, cols = saved.shape
    step = 16
    return pl.pallas_call(
        functools.partial(spawn_kernel, months, ages, total_ages),
        grid=(rows // step,),
        in_specs=[
            whole(SMEM),
            whole(SMEM),
            pl.BlockSpec((months, ages, step, cols), lambda i: (0, 0, i, 0)),
            pl.BlockSpec((step, cols), lambda i: (i, 0)),
            pl.BlockSpec(memory_space=pl.ANY),
        ],
        out_specs=pl.BlockSpec((months + 1, step, cols), lambda i: (0, i, 0)),
        out_shape=jax.ShapeDtypeStruct((months + 1, rows, cols), f32),
        compiler_params=params_of(SPAWN_MB),
        name="spawn_parts",
    )(pos, breeding, saved, first, ahead_of)


def add_kernel(a_ref, b_ref, _, out_ref):
    out_ref[...] = a_ref[...] + b_ref[...]


def add_after(a, b, ahead_of):
    return pl.pallas_call(
        add_kernel,
        in_specs=[whole(), whole(), pl.BlockSpec(memory_space=pl.ANY)],
        out_specs=whole(),
        out_shape=jax.ShapeDtypeStruct(a.shape, a.dtype),
        compiler_params=params_of(8),
        name="add_after",
    )(a, b, ahead_of)


def flipped(x, axis, reach):
    return lax.ppermute(x, axis, [(i, i ^ reach) for i in range(lax.axis_size(axis))])


def first_terms(x, axis):
    n = lax.axis_size(axis)
    if n & (n - 1):
        return [x] + [shift(x, axis, d) for d in range(1, n)]
    return [x, flipped(x, axis, 1)] if n > 1 else [x]


def other_terms(terms, axis, ahead_of):
    n = lax.axis_size(axis)
    if n & (n - 1):
        return terms
    reach = 2
    while reach < n:
        mine = add_after(*terms, ahead_of)
        terms = [mine, flipped(mine, axis, reach)]
        reach *= 2
    return terms


def pack_kernel(months, ages, sizes, fleets, *refs):
    pos_ref, fin_ref, next_ref, sea_ref, prey_ref, heat_ref = refs[:6]
    fleet_refs = refs[6 : 6 + fleets]
    death_ref, gear_ref, kappa_ref, tau_ref, ideal_ref, breed_ref = refs[6 + fleets : 12 + fleets]
    ahead_ref, back_ref, east_ref, west_ref, fleet_out, later_ref, table_ref, openv, openh, forage, heat4 = refs[12 + fleets :]
    n_coh, n_lat, n_lon = sizes
    age = lax.broadcasted_iota(jnp.int32, (1, ages), 1) + (pos_ref[0] * ages + 1)
    table_ref[...] = jnp.zeros_like(table_ref)
    table_ref[DEATH : DEATH + 1, 0:ages] = death_ref[...] * -LOG2E
    table_ref[GEAR2 : GEAR2 + 1, 0:ages] = gear_ref[...] * LOG2E
    table_ref[KAPPA : KAPPA + 1, 0:ages] = kappa_ref[...]
    table_ref[TAU : TAU + 1, 0:ages] = tau_ref[...]
    table_ref[IDEAL : IDEAL + 1, 0:ages] = ideal_ref[...] * 0.25
    table_ref[MAT : MAT + 1, 0:ages] = age.astype(f32) / (ages * n_coh) * breed_ref[...]
    table_ref[GEAR : GEAR + 1, 0:ages] = gear_ref[...]
    rows, cols = next_ref.shape
    keep = (pos_ref[0] < n_coh - 1).astype(f32)
    last = next_ref[...] * keep
    later_ref[...] = last

    count = fleet_refs[0].shape[0]
    half = count * fleets // 2
    for k, ref in enumerate(fleet_refs):
        at = k * count
        if count <= half:
            side, line = divmod(at, half)
            fleet_out[line : line + count, side * LANES : (side + 1) * LANES] = ref[...]
        else:
            fleet_out[0:half, 0:LANES] = ref[0:half, :]
            fleet_out[0:half, LANES : 2 * LANES] = ref[half:, :]

    band = 16
    for a in range(ages):
        if a + 1 < ages:
            top = fin_ref[a + 1, 0:band, :].astype(f32)[0:1]
            bottom = fin_ref[a + 1, rows - band : rows, :].astype(f32)[band - 1 : band]
        else:
            top, bottom = last[0:1], last[rows - 1 : rows]
        back_ref[a : a + 1, :] = top
        ahead_ref[a : a + 1, :] = bottom
    fields = [sea_ref[...].astype(f32)]
    for t in range(months):
        fields += [prey_ref[t], heat_ref[t]]
    for k, field in enumerate(fields):
        back_ref[ages + k : ages + k + 1, :] = field[0:1]
        ahead_ref[ages + k : ages + k + 1, :] = field[rows - 1 : rows]
    blank = jnp.zeros((1, cols), f32)
    start = up_to(ages + len(fields), SUB)
    for k in range(ages + len(fields), start):
        back_ref[k : k + 1, :] = blank
        ahead_ref[k : k + 1, :] = blank
    back_ref[start:, 0 : 2 * LANES] = fleet_out[...]
    ahead_ref[start:, 0 : 2 * LANES] = fleet_out[...]

    lane = lax.broadcasted_iota(jnp.int32, (rows, LANES), 1)
    east = jnp.zeros((rows, LANES), f32)
    west = jnp.zeros((rows, LANES), f32)
    for k in range(ages + len(fields)):
        if k + 1 < ages:
            left = fin_ref[k + 1, :, 0:LANES].astype(f32)
            right = fin_ref[k + 1, :, cols - LANES : cols].astype(f32)
        else:
            plane = last if k + 1 == ages else fields[k - ages]
            left, right = plane[:, 0:LANES], plane[:, cols - LANES : cols]
        west = jnp.where(lane == k, pltpu.roll(left, k, 1) if k else left, west)
        east = jnp.where(lane == k, pltpu.roll(right, k + 1, 1), east)
    east_ref[...] = east
    west_ref[...] = west

    sea = fields[0]
    line = lax.broadcasted_iota(jnp.int32, (rows, cols), 0)
    column = lax.broadcasted_iota(jnp.int32, (rows, cols), 1)
    openv[...] = jnp.where(line == rows - 1, 0.0, sea * pltpu.roll(sea, rows - 1, 0))
    openh[...] = jnp.where(column == cols - 1, 0.0, sea * pltpu.roll(sea, cols - 1, 1))
    for t in range(months):
        heat4[t] = heat_ref[t] * 0.25
        forage[t] = sea * prey_ref[t]


def relay_kernel(side, pos_ref, east_ref, west_ref, _, *refs):
    *block_refs, both_ref, gathered_ref = refs
    rows = east_ref.shape[0]
    at = 0
    for ref in block_refs:
        for half in range(2):
            gathered_ref[at : at + side, :] = ref[ref.shape[0] - side :, half * LANES : (half + 1) * LANES]
            at += side
    both_ref[0:rows, :] = jnp.where(pos_ref[2] == 0, east_ref[...], west_ref[...])
    both_ref[rows:, :] = gathered_ref[...]


def relay(pos, east, west, ahead_of, blocks, side):
    rows = east.shape[0]
    tall = 2 * side * len(blocks)
    return pl.pallas_call(
        functools.partial(relay_kernel, side),
        in_specs=[whole(SMEM), whole(), whole(), pl.BlockSpec(memory_space=pl.ANY)] + [whole()] * len(blocks),
        out_specs=[whole()] * 2,
        out_shape=[jax.ShapeDtypeStruct((rows + tall, LANES), f32), jax.ShapeDtypeStruct((tall, LANES), f32)],
        compiler_params=params_of(8),
        name="relay",
    )(pos, east, west, ahead_of, *blocks)


def pack_edges(sizes, pos, fin, nxt, sea, prey, heat, fleet_blocks, rates):
    ages, rows, cols = fin.shape
    months = prey.shape[0]
    half = len(fleet_blocks) * fleet_blocks[0].shape[0] // 2
    tall = up_to(ages + 1 + 2 * months, SUB) + half
    line = jax.ShapeDtypeStruct((tall, cols), f32)
    column = jax.ShapeDtypeStruct((rows, LANES), f32)
    return pl.pallas_call(
        functools.partial(pack_kernel, months, ages, sizes, len(fleet_blocks)),
        in_specs=[whole(SMEM)] + [whole()] * (5 + len(fleet_blocks) + len(rates)),
        out_specs=[whole()] * 11,
        out_shape=[
            line,
            line,
            column,
            column,
            jax.ShapeDtypeStruct((half, 2 * LANES), f32),
            jax.ShapeDtypeStruct((rows, cols), f32),
            jax.ShapeDtypeStruct((SUB, LANES), f32),
            jax.ShapeDtypeStruct((rows, cols), f32),
            jax.ShapeDtypeStruct((rows, cols), f32),
            jax.ShapeDtypeStruct((months, rows, cols), f32),
            jax.ShapeDtypeStruct((months, rows, cols), f32),
        ],
        compiler_params=params_of(16),
        name="pack_edges",
    )(pos, fin, nxt, sea, prey, heat, *fleet_blocks, *[rate.reshape(1, ages) for rate in rates])


def recruit_kernel(c, terms, *refs):
    pos_ref, par_ref, parv_ref, sea_ref, yield_ref, fish_ref, nxt_ref = refs[:7]
    term_refs = refs[7 : 7 + terms]
    rowc, colw, cole, catch, _ = refs[7 + terms : 12 + terms]
    all_ref, ahead_out, back_out, east_out, west_out, both_out, recruit_out, last_out, top, bottom = refs[12 + terms :]
    rows, cols, ages, months = c.rows, c.cols, c.ages, c.months
    n_i, n_j = rows // SUB, cols // LANES
    keep = (pos_ref[0] < c.sizes[0] - 1).astype(f32)
    spawning = functools.reduce(jnp.add, [r[c.month] for r in term_refs])
    first = functools.reduce(jnp.add, [r[months] for r in term_refs])
    ratio = 1.0 / (1.0 + spawning)
    recruit_out[...] = first * sea_ref[...].astype(f32) * yield_ref[...] * ratio * ratio
    last = (nxt_ref[0:rows, :] + recruit_out[...] * nxt_ref[rows : rows + 1, :]) * keep
    last_out[...] = last

    def body(h, carry):
        for k in range(BATCH):
            a = h * BATCH + k
            mat = par_ref[MAT, a]
            for i in range(n_i):
                for j in range(n_j):
                    ys, xs = slice(i * SUB, (i + 1) * SUB), slice(j * LANES, (j + 1) * LANES)
                    value = at_edges(
                        c, i, j, a, all_ref[a, ys, xs], fish_ref, rowc, colw, cole, catch.at[c.month]
                    )
                    value = value + recruit_out[ys, xs] * mat
                    all_ref[a, ys, xs] = value
                    if i == 0:
                        top[j, pl.ds(a, 1), :] = value[0:1]
                    if i == n_i - 1:
                        bottom[j, pl.ds(a, 1), :] = value[SUB - 1 : SUB]
        return carry

    lax.fori_loop(0, ages // BATCH, body, 0)
    place = lax.broadcasted_iota(jnp.int32, (ages, cols), 0)
    for src, dst, row in ((top, back_out, 0), (bottom, ahead_out, rows - 1)):
        full = jnp.concatenate([src[j] for j in range(n_j)], axis=1)
        dst[...] = jnp.where(place == ages - 1, last[row : row + 1, :], pltpu.roll(full, ages - 1, 0))
    lane = lax.broadcasted_iota(jnp.int32, (SUB, LANES), 1)
    for i in range(n_i):
        rs = slice(i * SUB, (i + 1) * SUB)
        for dst, lo, by, col in ((west_out, 0, 0, 0), (east_out, cols - LANES, 1, cols - 1)):
            found = jnp.where(lane == ages - 1, last_out[rs, col : col + 1], 0.0)
            for k in range(1, ages):
                value = all_ref[k, rs, lo : lo + LANES]
                found = jnp.where(lane == k - 1, pltpu.roll(value, k - 1 + by, 1) if k - 1 + by else value, found)
            dst[rs, :] = found
    both_out[...] = jnp.where(pos_ref[2] == 0, east_out[...], west_out[...])


def recruit_edges(sizes, pos, par, sea, yields, fish, nxt, terms, edges, catch, inner):
    ages, rows, cols = inner.shape
    months = terms[0].shape[0] - 1
    c = Cfg(rows=rows, cols=cols, ages=ages, months=months, month=months - 1, sizes=sizes)
    line = jax.ShapeDtypeStruct((ages, cols), f32)
    column = jax.ShapeDtypeStruct((rows, LANES), f32)
    operands = [pos, par, par, sea, yields, fish, nxt, *terms, *edges, catch, inner]
    return pl.pallas_call(
        functools.partial(recruit_kernel, c, len(terms)),
        in_specs=[whole(SMEM), whole(SMEM)] + [whole()] * (len(operands) - 2),
        out_specs=[whole()] * 8,
        out_shape=[jax.ShapeDtypeStruct(inner.shape, f32), line, line, column, column, column]
        + [jax.ShapeDtypeStruct((rows, cols), f32)] * 2,
        scratch_shapes=[pltpu.VMEM((cols // LANES, ages, LANES), f32)] * 2,
        input_output_aliases={len(operands) - 1: 0},
        cost_estimate=pl.CostEstimate(flops=16 * inner.size, bytes_accessed=8 * inner.size, transcendentals=0),
        compiler_params=params_of(8),
        name="recruit_edges",
    )(*operands)


class Cfg:
    def __init__(self, **kw):
        self.__dict__.update(kw)


def column_of(par_ref, k, ages):
    down = lax.broadcasted_iota(jnp.int32, (ages, LANES), 0)
    across = lax.broadcasted_iota(jnp.int32, (ages, LANES), 1)
    row = jnp.broadcast_to(par_ref[k : k + 1, :], (ages, LANES))
    return jnp.sum(jnp.where(down == across, row, 0.0), axis=1, keepdims=True)


def edge_flux(c, pos_ref, parv_ref, sea_ref, forage_ref, heat4_ref, own, got, msgs, rowc, colw, cole, fish_ref=None):
    rows, cols, ages = c.rows, c.cols, c.ages
    n_coh, n_lat, n_lon = c.sizes
    own_ahead, own_back, own_east, own_west = own
    from_before, from_after, from_west, from_east = got
    msg_before, msg_after, msg_west, msg_east = msgs
    sea_line, prey_line, heat_line = ages, ages + 1 + 2 * c.month, ages + 2 + 2 * c.month
    kappa, tau, ideal, death, gear2 = (column_of(parv_ref, k, ages) for k in (KAPPA, TAU, IDEAL, DEATH, GEAR2))
    has = [
        (pos_ref[1] > 0).astype(f32),
        (pos_ref[1] < n_lat - 1).astype(f32),
        (pos_ref[2] > 0).astype(f32),
        (pos_ref[2] < n_lon - 1).astype(f32),
    ]
    for k, (row, own, got, msg) in enumerate(
        ((0, own_back, from_before, msg_before), (rows - 1, own_ahead, from_after, msg_after))
    ):
        here = habitat_of(forage_ref[row : row + 1, :], heat4_ref[row : row + 1, :], ideal, tau)
        sea_there = msg[sea_line : sea_line + 1, :]
        there = habitat_of(
            sea_there * msg[prey_line : prey_line + 1, :], msg[heat_line : heat_line + 1, :] * 0.25, ideal, tau
        )
        both = sea_ref[row : row + 1, :].astype(f32) * sea_there * has[k]
        flux = both * (kappa + jnp.maximum(there - here, 0.0)) * (own[0:ages, :] - got[0:ages, :])
        if fish_ref is not None:
            flux = flux * jnp.exp2(death - gear2 * fish_ref[row : row + 1, :])
        for j in range(cols // LANES):
            rowc[k, j] = flux[:, j * LANES : (j + 1) * LANES]
    kappa, tau, ideal, death, gear2 = (parv_ref[k : k + 1, :] for k in (KAPPA, TAU, IDEAL, DEATH, GEAR2))
    for k, (col, own, got, msg, dst) in enumerate(
        ((0, own_west, from_west, msg_west, colw), (cols - 1, own_east, from_east, msg_east, cole))
    ):
        here = habitat_of(forage_ref[:, col : col + 1], heat4_ref[:, col : col + 1], ideal, tau)
        msg = msg.at[0:rows]
        sea_there = msg[:, sea_line : sea_line + 1]
        there = habitat_of(
            sea_there * msg[:, prey_line : prey_line + 1], msg[:, heat_line : heat_line + 1] * 0.25, ideal, tau
        )
        both = sea_ref[:, col : col + 1].astype(f32) * sea_there * has[2 + k]
        flux = both * (kappa + jnp.maximum(there - here, 0.0)) * (own[0:rows, :] - got[0:rows, :])
        if fish_ref is not None:
            flux = flux * jnp.exp2(death - gear2 * fish_ref[:, col : col + 1])
        dst[...] = flux


def advance(c, k, a, par_ref, load, tables, out_ref, recruit=None):
    openv, openh, forage, heat4, fish_ref, *edges = tables
    if edges:
        rowc, colw, cole, catch = edges
    n_i, n_j = c.rows // SUB, c.cols // LANES
    lane = lax.broadcasted_iota(jnp.int32, (SUB, LANES), 1)
    sub = lax.broadcasted_iota(jnp.int32, (SUB, LANES), 0)
    kappa, tau, ideal = par_ref[KAPPA, a], par_ref[TAU, a], par_ref[IDEAL, a]
    death, gear2 = par_ref[DEATH, a], par_ref[GEAR2, a]
    if recruit is not None:
        mat = par_ref[MAT, a]

    def tile(i, j):
        return slice(i * SUB, (i + 1) * SUB), slice(j * LANES, (j + 1) * LANES)

    def strip(i):
        adj, hab = [], []
        for j in range(n_j):
            at = tile(i, j)
            adj.append(load(*at))
            off = heat4[at] - ideal
            hab.append(forage[at] * tau * pl.reciprocal(1.0 + off * off, approx=False))
        return adj, hab, [pltpu.roll(v, SUB - 1, 0) for v in adj], [pltpu.roll(v, SUB - 1, 0) for v in hab]

    now = strip(0)
    above = [jnp.zeros((SUB, LANES), f32)] * n_j
    if edges:
        above = [jnp.broadcast_to(-rowc[0, j, pl.ds(a, 1), :], (SUB, LANES)) for j in range(n_j)]
        below = [jnp.broadcast_to(rowc[1, j, pl.ds(a, 1), :], (SUB, LANES)) for j in range(n_j)]
    for i in range(n_i):
        after = strip(i + 1) if i + 1 < n_i else now
        adj, hab, adj_up, hab_up = now
        out = [None] * n_j
        for j in range(n_j):
            at = tile(i, j)
            adj_d = jnp.where(sub == SUB - 1, after[2][j], adj_up[j])
            hab_d = jnp.where(sub == SUB - 1, after[3][j], hab_up[j])
            g = hab_d - hab[j]
            d = openv[at] * (adj[j] - adj_d)
            p = jnp.maximum(g, 0.0) + kappa
            f = p * d
            if edges and i == n_i - 1:
                f = jnp.where(sub == SUB - 1, below[j], f)
            turned = pltpu.roll((p - g) * d, 1, 0)
            out[j] = f - jnp.where(sub == 0, above[j], turned)
            above[j] = turned
        adj_l = [pltpu.roll(v, LANES - 1, 1) for v in adj]
        hab_l = [pltpu.roll(v, LANES - 1, 1) for v in hab]
        flows, backs = [], []
        for j in range(n_j):
            at = tile(i, j)
            if j + 1 < n_j:
                adj_d = jnp.where(lane == LANES - 1, adj_l[j + 1], adj_l[j])
                hab_d = jnp.where(lane == LANES - 1, hab_l[j + 1], hab_l[j])
            else:
                adj_d, hab_d = adj_l[j], hab_l[j]
            g = hab_d - hab[j]
            d = openh[at] * (adj[j] - adj_d)
            p = jnp.maximum(g, 0.0) + kappa
            flows.append(p * d)
            backs.append(pltpu.roll((p - g) * d, 1, 1))
        rs = slice(i * SUB, (i + 1) * SUB)
        if edges:
            edge_e = pltpu.roll(cole[rs, :], (2 * LANES - 1) - a, 1)
            edge_w = pltpu.roll(-colw[rs, :], LANES - a, 1)
            flows[-1] = jnp.where(lane == LANES - 1, edge_e, flows[-1])
        else:
            edge_w = jnp.zeros((SUB, LANES), f32)
        for j in range(n_j):
            at = tile(i, j)
            came = jnp.where(lane == 0, backs[j - 1] if j else edge_w, backs[j])
            moved = adj[j] - (out[j] + flows[j] - came)
            fish = fish_ref[at]
            survive = jnp.exp2(death - gear2 * fish)
            value = survive * moved
            if edges:
                value = value + fish * catch[i * SUB // BY, j, pl.ds(a, 1), :]
            if recruit is not None:
                value = value + recruit[at] * mat
            out_ref[(k,) + at] = value
        now = after


def at_edges(c, i, j, a, value, fish_ref, rowc, colw, cole, catch):
    lane = lax.broadcasted_iota(jnp.int32, (SUB, LANES), 1)
    sub = lax.broadcasted_iota(jnp.int32, (SUB, LANES), 0)
    rs = slice(i * SUB, (i + 1) * SUB)
    n_i, n_j = c.rows // SUB, c.cols // LANES
    value = value + fish_ref[rs, j * LANES : (j + 1) * LANES] * catch[i * SUB // BY, j, pl.ds(a, 1), :]
    if i == 0:
        value = value - jnp.where(sub == 0, rowc[0, j, pl.ds(a, 1), :], 0.0)
    if i == n_i - 1:
        value = value - jnp.where(sub == SUB - 1, rowc[1, j, pl.ds(a, 1), :], 0.0)
    if j == 0:
        value = value - jnp.where(lane == 0, pltpu.roll(colw[rs, :], LANES - a, 1), 0.0)
    if j == n_j - 1:
        value = value - jnp.where(lane == LANES - 1, pltpu.roll(cole[rs, :], (2 * LANES - 1) - a, 1), 0.0)
    return value


def read_plane(ref, k, ys, xs):
    if ref.dtype == f32:
        return ref[k, ys, xs]
    low = ys.start // 16 * 16
    wide = ref[k, low : low + 16, xs].astype(f32)
    return wide[ys.start - low : ys.stop - low]


def all_cohorts(c, step, count, par_ref, later_ref, next_ref, recruit_ref, go):
    def loader(a):
        def load(ys, xs):
            value = read_plane(later_ref, a + 1, ys, xs)
            if recruit_ref is not None:
                value = value + recruit_ref[ys, xs] * par_ref[MAT, a + 1]
            return value

        return load

    def body(h, carry):
        for k in range(PAIR):
            go(h * PAIR + k, step * count + h * PAIR + k, loader(step * count + h * PAIR + k))
        return carry

    final = step == c.ages // count - 1
    turns = count // PAIR
    fixed = isinstance(step, int)
    if fixed:
        lax.fori_loop(0, turns - 1 if final else turns, body, 0)
    else:
        lax.fori_loop(0, jnp.where(final, turns - 1, turns), body, 0)

    def rest():
        for k in range(count - PAIR, count):
            a = c.ages - count + k
            go(k, a, loader(a) if a + 1 < c.ages else lambda ys, xs: next_ref[ys, xs])

    if not fixed:
        pl.when(final)(rest)
    elif final:
        rest()


def first_kernel(c, *refs):
    refs = list(refs)

    def take(n):
        out = refs[:n]
        del refs[:n]
        return out

    pos_ref, parv_ref, inner_ref = take(3)
    own, got = take(4), take(4)
    sea_ref, fish_ref = take(2)
    fleet_refs = take(c.n_fleet)
    forage, heat4 = take(2)
    plane_out, rowc, colw, cole, catch = take(5)
    rows, cols, ages, months = c.rows, c.cols, c.ages, c.months
    blocks_y, blocks_x = rows // BY, cols // BX
    edge_flux(c, pos_ref, parv_ref, sea_ref, forage.at[c.month], heat4.at[c.month], own, got, got, rowc, colw, cole, fish_ref)

    flat = jnp.concatenate([ref[...] for ref in fleet_refs], axis=0)
    names = flat[:, months * ages : months * ages + 1]
    turned = flat.T[0 : months * ages]
    base = ((pos_ref[1] * c.sizes[2] + pos_ref[2]) * (blocks_y * blocks_x)).astype(f32)
    block_col = (lax.broadcasted_iota(jnp.int32, (flat.shape[0], cols), 1) // BX).astype(f32)
    gear = column_of(parv_ref, GEAR, ages)
    for by in range(blocks_y):
        named = (block_col == names - (base + by * blocks_x)).astype(f32)
        sums = jnp.dot(turned, named, precision=lax.Precision.HIGHEST, preferred_element_type=f32)
        for t in range(months):
            for j in range(cols // LANES):
                catch[t, by, j] = gear * sums[t * ages : (t + 1) * ages, j * LANES : (j + 1) * LANES]

    for i in range(rows // SUB):
        for j in range(cols // LANES):
            ys, xs = slice(i * SUB, (i + 1) * SUB), slice(j * LANES, (j + 1) * LANES)
            plane_out[0, ys, xs] = at_edges(
                c, i, j, 0, inner_ref[0, ys, xs], fish_ref, rowc, colw, cole, catch.at[c.month]
            )
    plane_out[0, rows : rows + SUB, :] = jnp.broadcast_to(
        jnp.broadcast_to(parv_ref[MAT : MAT + 1, 0:1], (1, cols)), (SUB, cols)
    )


def month_kernel(c, *refs):
    par_ref, later_ref, next_ref, fish_ref, openv, openh, forage, heat4 = refs[:8]
    out_ref = refs[-1]
    tables = (openv, openh, forage.at[c.month], heat4.at[c.month], fish_ref)

    def go(k, a, load):
        advance(c, a, a, par_ref, load, tables, out_ref)

    all_cohorts(c, c.part, c.ages // PARTS, par_ref, later_ref, next_ref, None, go)


def last_kernel(c, *refs):
    refs = list(refs)

    def take(n):
        out = refs[:n]
        del refs[:n]
        return out

    pos_ref, par_ref, parv_ref, later_ref, next_ref, recruit_ref, sea_ref, fish_ref, yield_ref = take(9)
    openv, openh, forage, heat4, catch = take(5)
    own, got, msgs = take(4), take(4), take(4)
    term_refs = take(c.n_terms)
    bcast_refs = take(c.n_bcast)
    out_ref, grad_ref = take(2)
    rowc, colw, cole, final_recruit = take(4)
    rows, months = c.rows, c.months
    step = pl.program_id(0)

    @pl.when(step == 0)
    def _():
        edge_flux(
            c, pos_ref, parv_ref, sea_ref, forage.at[c.month], heat4.at[c.month], own, got, msgs, rowc, colw, cole
        )
        sea = sea_ref[...].astype(f32)
        totals = [functools.reduce(jnp.add, [r[t] for r in term_refs]) for t in range(months + 1)]
        first = bcast_refs[0][...] * (pos_ref[0] == 0).astype(f32)
        first = first + bcast_refs[1][...] * (pos_ref[0] == c.sizes[0] - 1).astype(f32)
        for ref in bcast_refs[2:]:
            first = first + ref[...]
        first = first[0:rows] + recruit_ref[...] * first[rows : rows + 1]
        ratios = [1.0 / (1.0 + totals[t]) for t in range(months)]
        grad_ref[...] = (totals[months] * totals[1] * ratios[1] + first * totals[0] * ratios[0]) * sea
        final_recruit[...] = first * sea * yield_ref[...] * ratios[0] * ratios[0]

    tables = (openv, openh, forage.at[c.month], heat4.at[c.month], fish_ref, rowc, colw, cole, catch.at[c.month])

    def go(k, a, load):
        advance(c, k, a, par_ref, load, tables, out_ref, recruit=final_recruit)

    all_cohorts(c, step, GROUP, par_ref, later_ref, next_ref, None, go)


def cost(planes, rows, cols):
    cells = planes * rows * cols
    return pl.CostEstimate(flops=60 * cells, bytes_accessed=8 * cells, transcendentals=2 * cells)


def edge_shapes(ages, rows, cols):
    return [
        jax.ShapeDtypeStruct((2, cols // LANES, ages, LANES), f32),
        jax.ShapeDtypeStruct((rows, LANES), f32),
        jax.ShapeDtypeStruct((rows, LANES), f32),
    ]


def first_cohort(sizes, pos, par, inner, own, got, sea, fish, fleet_blocks, forage, heat4):
    ages, rows, cols = inner.shape
    months = forage.shape[0]
    c = Cfg(rows=rows, cols=cols, ages=ages, months=months, month=months - 1, sizes=sizes, n_fleet=len(fleet_blocks))
    operands = [pos, par, inner, *own, *got, sea, fish]
    at = len(operands)
    operands += [block for block, _ in fleet_blocks] + [forage, heat4]

    def kernel(*refs):
        refs = list(refs)
        for k, (block, start) in enumerate(fleet_blocks):
            if start:
                refs[at + k] = refs[at + k].at[start : block.shape[0]]
        first_kernel(c, *refs)

    out_shape = [jax.ShapeDtypeStruct((1, rows + SUB, cols), f32)]
    out_shape += edge_shapes(ages, rows, cols)
    out_shape.append(jax.ShapeDtypeStruct((months, rows // BY, cols // LANES, ages, LANES), f32))
    return pl.pallas_call(
        kernel,
        in_specs=[whole(SMEM)] + [whole()] * (len(operands) - 1),
        out_specs=[whole()] * len(out_shape),
        out_shape=out_shape,
        cost_estimate=cost(4, rows, cols),
        compiler_params=params_of(8),
        name="first_cohort",
    )(*operands)


def month_inner(sizes, part, par, fin, nxt, fish, fields, before, ahead_of):
    ages, rows, cols = fin.shape
    months = fields[2].shape[0]
    c = Cfg(rows=rows, cols=cols, ages=ages, months=months, month=months - 1, sizes=sizes, part=part)
    operands = [par, fin, nxt, fish, *fields, ahead_of]
    specs = [whole(SMEM)] + [whole()] * (len(operands) - 2) + [pl.BlockSpec(memory_space=pl.ANY)]
    alias = {}
    if before is not None:
        alias = {len(operands): 0}
        operands.append(before)
        specs.append(whole())
    return pl.pallas_call(
        functools.partial(month_kernel, c),
        in_specs=specs,
        out_specs=whole(),
        out_shape=jax.ShapeDtypeStruct((ages, rows, cols), f32),
        input_output_aliases=alias,
        cost_estimate=cost(ages // PARTS, rows, cols),
        compiler_params=params_of(16),
        name="month_inner",
    )(*operands)


def month_last(sizes, pos, par, later, nxt, recruit, sea, fish, yields, fields, catch, own, got, msgs, terms, bcasts):
    ages, rows, cols = later.shape
    months = catch.shape[0]
    c = Cfg(
        rows=rows, cols=cols, ages=ages, months=months, month=0, sizes=sizes, n_terms=len(terms), n_bcast=len(bcasts)
    )
    operands = [pos, par, par, later, nxt, recruit, sea, fish, yields, *fields, catch, *own, *got, *msgs]
    operands += [*terms, *bcasts]
    scratch = [pltpu.VMEM(x.shape, f32) for x in edge_shapes(ages, rows, cols)]
    return pl.pallas_call(
        functools.partial(last_kernel, c),
        grid=(ages // GROUP,),
        in_specs=[whole(SMEM), whole(SMEM)] + [whole()] * (len(operands) - 2),
        out_specs=[pl.BlockSpec((GROUP, rows, cols), lambda i: (i, 0, 0)), whole()],
        out_shape=[jax.ShapeDtypeStruct((ages, rows, cols), f32), jax.ShapeDtypeStruct((rows, cols), f32)],
        scratch_shapes=scratch + [pltpu.VMEM((rows, cols), f32)],
        cost_estimate=cost(ages, rows, cols),
        compiler_params=params_of(16),
        name="month_last",
    )(*operands)


def habitat_of(forage, heat, ideal, tau):
    off = heat - ideal
    return forage * (tau / (1.0 + off * off))


def shards(
    saved,
    fin,
    prey,
    heat,
    sea,
    fish,
    yields,
    death,
    gear,
    kappa,
    tau,
    ideal,
    breeding,
    landing,
    east_piece,
    north_piece,
    patch,
    bounds,
):
    months, ages, rows, cols = saved.shape
    n_coh, n_lat, n_lon = sizes = tuple(lax.axis_size(axis) for axis in ("coh", "lat", "lon"))
    at_coh, at_lat, at_lon = (lax.axis_index(axis) for axis in ("coh", "lat", "lon"))
    pos = jnp.stack([at_coh, at_lat, at_lon]).astype(jnp.int32)
    cohort_age = at_coh * ages + jnp.arange(ages)
    nblocks = (rows // BY) * (cols // BX)
    inside = (cohort_age[None, :] >= bounds[:, 0:1]) & (cohort_age[None, :] < bounds[:, 1:2])
    masked = (landing * inside[:, None, :].astype(f32)).reshape(landing.shape[0], months * ages)
    names = ((north_piece * n_lon + east_piece[:, 0]) * nblocks + patch).astype(f32)
    fleet = jnp.concatenate([masked, names[:, None]], axis=1)
    fleet = jnp.pad(fleet, ((0, 0), (0, LANES - fleet.shape[1])))

    first = fin[0].astype(f32)
    nxt = shift(first, "coh", -1)
    terms = first_terms(spawn_parts(pos, breeding, ages * n_coh, saved, first, first), "coh")

    ahead, back, east, west, fleet_pack, later_last, par, *fields = pack_edges(
        sizes, pos, fin, nxt, sea, prey, heat, [fleet], (death, gear, kappa, tau, ideal, breeding)
    )
    from_before, from_after = shift(ahead, "lat", 1), shift(back, "lat", -1)
    blocks = [ahead, from_before] + ([from_after] if n_lat > 2 else [])
    blocks += [shift(fleet_pack, "lat", d) for d in range(2, n_lat - 1)]
    inner = month_inner(sizes, 0, par, fin, later_last, fish, fields, None, ahead)
    both, gathered = relay(pos, east, west, inner, blocks, fleet_pack.shape[0])
    terms = other_terms(terms, "coh", both)
    inner = month_inner(sizes, 1, par, fin, later_last, fish, fields, inner, both)
    from_west, from_east = swap_edges(east, west, both, "lon")
    fleet_blocks = [(gathered, 0)]
    if n_lon == 2:
        fleet_blocks.append((from_west, rows))
    else:
        fleet_blocks += [(shift(gathered, "lon", d), 0) for d in range(1, n_lon)]
    own = (ahead, back, east, west)
    msgs = (from_before, from_after, from_west, from_east)
    plane, *edges, catch = first_cohort(
        sizes, pos, par, inner, own, msgs, sea, fish, fleet_blocks, fields[2], fields[3]
    )
    plane = plane.reshape(rows + SUB, cols)
    down = shift(plane, "coh", -1)
    bcasts = [plane, down] + [lax.ppermute(plane, "coh", [(0, j)]) for j in range(1, n_coh - 1)]
    later, ahead, back, east, west, both, recruit, nxt = recruit_edges(
        sizes, pos, par, sea, yields, fish, down, terms, edges, catch, inner
    )
    own = (ahead, back, east, west)
    got = (shift(ahead, "lat", 1), shift(back, "lat", -1), *swap_edges(east, west, both, "lon"))
    return tuple(
        month_last(
            sizes, pos, par, later, nxt, recruit, sea, fish, yields, fields, catch, own, got, msgs, terms, bcasts
        )
    )


def solution(mesh):
    in_specs = (
        P(None, "coh", "lat", "lon"),
        P("coh", "lat", "lon"),
        P(None, "lat", "lon"),
        P(None, "lat", "lon"),
        P("lat", "lon"),
        P("lat", "lon"),
        P("lat", "lon"),
        P("coh"),
        P("coh"),
        P("coh"),
        P("coh"),
        P("coh"),
        P("coh"),
        P(("lat", "lon"), None, "coh"),
        P(("lat", "lon"), None),
        P(("lat", "lon")),
        P(("lat", "lon")),
        P(("lat", "lon"), None),
    )
    out_specs = (P("coh", "lat", "lon"), P("lat", "lon"))

    return jax.shard_map(shards, mesh=mesh, in_specs=in_specs, out_specs=out_specs, check_vma=False)
```

```python
import functools
import math

import jax
import jax.numpy as jnp
from jax import lax
from jax.experimental import pallas as pl
from jax.experimental.pallas import tpu as pltpu
from jax.sharding import PartitionSpec as P

BY = 16
BX = 32
LANES = 128
SUB = 8
GROUP = 8
PAIR = 2
PARTS = 2
BATCH = 16
SPAWN_MB = 24

f32 = jnp.float32
VMEM = pltpu.MemorySpace.VMEM
SMEM = pltpu.MemorySpace.SMEM
LOG2E = math.log2(math.e)

DEATH, GEAR2, KAPPA, TAU, IDEAL, MAT, GEAR = range(7)


def up_to(value, step):
    return -(-value // step) * step


def whole(memory=VMEM):
    return pl.BlockSpec(memory_space=memory)


def params_of(limit=48):
    return pltpu.CompilerParams(vmem_limit_bytes=limit * 2**20)


def shift(x, axis, distance):
    n = lax.axis_size(axis)
    return lax.ppermute(x, axis, [(i, (i + distance) % n) for i in range(n)])


def swap_edges(ahead, back, both, axis):
    n = lax.axis_size(axis)
    if n == 1:
        return ahead, back
    if n == 2:
        got = shift(both, axis, 1)
        return got, got
    return shift(ahead, axis, 1), shift(back, axis, -1)


def spawn_kernel(months, ages, total_ages, pos_ref, breed_ref, saved_ref, first_ref, _, out_ref):
    mat = [(pos_ref[0] * ages + (a + 1)).astype(f32) / total_ages * breed_ref[a] for a in range(ages)]
    for t in range(months):
        total = saved_ref[t, 0].astype(f32) * mat[0]
        for a in range(1, ages):
            total = total + saved_ref[t, a].astype(f32) * mat[a]
        out_ref[t] = total
    youngest = (pos_ref[0] == 0).astype(f32)
    out_ref[months] = first_ref[...] * youngest


def spawn_parts(pos, breeding, total_ages, saved, first, ahead_of):
    months, ages, rows, cols = saved.shape
    step = 16
    return pl.pallas_call(
        functools.partial(spawn_kernel, months, ages, total_ages),
        grid=(rows // step,),
        in_specs=[
            whole(SMEM),
            whole(SMEM),
            pl.BlockSpec((months, ages, step, cols), lambda i: (0, 0, i, 0)),
            pl.BlockSpec((step, cols), lambda i: (i, 0)),
            pl.BlockSpec(memory_space=pl.ANY),
        ],
        out_specs=pl.BlockSpec((months + 1, step, cols), lambda i: (0, i, 0)),
        out_shape=jax.ShapeDtypeStruct((months + 1, rows, cols), f32),
        compiler_params=params_of(SPAWN_MB),
        name="spawn_parts",
    )(pos, breeding, saved, first, ahead_of)


def add_kernel(a_ref, b_ref, _, out_ref):
    out_ref[...] = a_ref[...] + b_ref[...]


def add_after(a, b, ahead_of):
    return pl.pallas_call(
        add_kernel,
        in_specs=[whole(), whole(), pl.BlockSpec(memory_space=pl.ANY)],
        out_specs=whole(),
        out_shape=jax.ShapeDtypeStruct(a.shape, a.dtype),
        compiler_params=params_of(8),
        name="add_after",
    )(a, b, ahead_of)


def flipped(x, axis, reach):
    return lax.ppermute(x, axis, [(i, i ^ reach) for i in range(lax.axis_size(axis))])


def first_terms(x, axis):
    n = lax.axis_size(axis)
    if n & (n - 1):
        return [x] + [shift(x, axis, d) for d in range(1, n)]
    return [x, flipped(x, axis, 1)] if n > 1 else [x]


def other_terms(terms, axis, ahead_of):
    n = lax.axis_size(axis)
    if n & (n - 1):
        return terms
    reach = 2
    while reach < n:
        mine = add_after(*terms, ahead_of)
        terms = [mine, flipped(mine, axis, reach)]
        reach *= 2
    return terms


def pack_kernel(months, ages, sizes, fleets, *refs):
    pos_ref, fin_ref, next_ref, sea_ref, prey_ref, heat_ref = refs[:6]
    fleet_refs = refs[6 : 6 + fleets]
    death_ref, gear_ref, kappa_ref, tau_ref, ideal_ref, breed_ref = refs[6 + fleets : 12 + fleets]
    ahead_ref, back_ref, east_ref, west_ref, fleet_out, later_ref, table_ref, openv, openh, forage, heat4 = refs[12 + fleets :]
    n_coh, n_lat, n_lon = sizes
    age = lax.broadcasted_iota(jnp.int32, (1, ages), 1) + (pos_ref[0] * ages + 1)
    table_ref[...] = jnp.zeros_like(table_ref)
    table_ref[DEATH : DEATH + 1, 0:ages] = death_ref[...] * -LOG2E
    table_ref[GEAR2 : GEAR2 + 1, 0:ages] = gear_ref[...] * LOG2E
    table_ref[KAPPA : KAPPA + 1, 0:ages] = kappa_ref[...]
    table_ref[TAU : TAU + 1, 0:ages] = tau_ref[...]
    table_ref[IDEAL : IDEAL + 1, 0:ages] = ideal_ref[...] * 0.25
    table_ref[MAT : MAT + 1, 0:ages] = age.astype(f32) / (ages * n_coh) * breed_ref[...]
    table_ref[GEAR : GEAR + 1, 0:ages] = gear_ref[...]
    rows, cols = next_ref.shape
    keep = (pos_ref[0] < n_coh - 1).astype(f32)
    last = next_ref[...] * keep
    later_ref[...] = last

    count = fleet_refs[0].shape[0]
    half = count * fleets // 2
    for k, ref in enumerate(fleet_refs):
        at = k * count
        if count <= half:
            side, line = divmod(at, half)
            fleet_out[line : line + count, side * LANES : (side + 1) * LANES] = ref[...]
        else:
            fleet_out[0:half, 0:LANES] = ref[0:half, :]
            fleet_out[0:half, LANES : 2 * LANES] = ref[half:, :]

    band = 16
    for a in range(ages):
        if a + 1 < ages:
            top = fin_ref[a + 1, 0:band, :].astype(f32)[0:1]
            bottom = fin_ref[a + 1, rows - band : rows, :].astype(f32)[band - 1 : band]
        else:
            top, bottom = last[0:1], last[rows - 1 : rows]
        back_ref[a : a + 1, :] = top
        ahead_ref[a : a + 1, :] = bottom
    fields = [sea_ref[...].astype(f32)]
    for t in range(months):
        fields += [prey_ref[t], heat_ref[t]]
    for k, field in enumerate(fields):
        back_ref[ages + k : ages + k + 1, :] = field[0:1]
        ahead_ref[ages + k : ages + k + 1, :] = field[rows - 1 : rows]
    blank = jnp.zeros((1, cols), f32)
    start = up_to(ages + len(fields), SUB)
    for k in range(ages + len(fields), start):
        back_ref[k : k + 1, :] = blank
        ahead_ref[k : k + 1, :] = blank
    back_ref[start:, 0 : 2 * LANES] = fleet_out[...]
    ahead_ref[start:, 0 : 2 * LANES] = fleet_out[...]

    lane = lax.broadcasted_iota(jnp.int32, (rows, LANES), 1)
    east = jnp.zeros((rows, LANES), f32)
    west = jnp.zeros((rows, LANES), f32)
    for k in range(ages + len(fields)):
        if k + 1 < ages:
            left = fin_ref[k + 1, :, 0:LANES].astype(f32)
            right = fin_ref[k + 1, :, cols - LANES : cols].astype(f32)
        else:
            plane = last if k + 1 == ages else fields[k - ages]
            left, right = plane[:, 0:LANES], plane[:, cols - LANES : cols]
        west = jnp.where(lane == k, pltpu.roll(left, k, 1) if k else left, west)
        east = jnp.where(lane == k, pltpu.roll(right, k + 1, 1), east)
    east_ref[...] = east
    west_ref[...] = west

    sea = fields[0]
    line = lax.broadcasted_iota(jnp.int32, (rows, cols), 0)
    column = lax.broadcasted_iota(jnp.int32, (rows, cols), 1)
    openv[...] = jnp.where(line == rows - 1, 0.0, sea * pltpu.roll(sea, rows - 1, 0))
    openh[...] = jnp.where(column == cols - 1, 0.0, sea * pltpu.roll(sea, cols - 1, 1))
    for t in range(months):
        heat4[t] = heat_ref[t] * 0.25
        forage[t] = sea * prey_ref[t]


def relay_kernel(side, pos_ref, east_ref, west_ref, _, *refs):
    *block_refs, both_ref, gathered_ref = refs
    rows = east_ref.shape[0]
    at = 0
    for ref in block_refs:
        for half in range(2):
            gathered_ref[at : at + side, :] = ref[ref.shape[0] - side :, half * LANES : (half + 1) * LANES]
            at += side
    both_ref[0:rows, :] = jnp.where(pos_ref[2] == 0, east_ref[...], west_ref[...])
    both_ref[rows:, :] = gathered_ref[...]


def relay(pos, east, west, ahead_of, blocks, side):
    rows = east.shape[0]
    tall = 2 * side * len(blocks)
    return pl.pallas_call(
        functools.partial(relay_kernel, side),
        in_specs=[whole(SMEM), whole(), whole(), pl.BlockSpec(memory_space=pl.ANY)] + [whole()] * len(blocks),
        out_specs=[whole()] * 2,
        out_shape=[jax.ShapeDtypeStruct((rows + tall, LANES), f32), jax.ShapeDtypeStruct((tall, LANES), f32)],
        compiler_params=params_of(8),
        name="relay",
    )(pos, east, west, ahead_of, *blocks)


def pack_edges(sizes, pos, fin, nxt, sea, prey, heat, fleet_blocks, rates):
    ages, rows, cols = fin.shape
    months = prey.shape[0]
    half = len(fleet_blocks) * fleet_blocks[0].shape[0] // 2
    tall = up_to(ages + 1 + 2 * months, SUB) + half
    line = jax.ShapeDtypeStruct((tall, cols), f32)
    column = jax.ShapeDtypeStruct((rows, LANES), f32)
    return pl.pallas_call(
        functools.partial(pack_kernel, months, ages, sizes, len(fleet_blocks)),
        in_specs=[whole(SMEM)] + [whole()] * (5 + len(fleet_blocks) + len(rates)),
        out_specs=[whole()] * 11,
        out_shape=[
            line,
            line,
            column,
            column,
            jax.ShapeDtypeStruct((half, 2 * LANES), f32),
            jax.ShapeDtypeStruct((rows, cols), f32),
            jax.ShapeDtypeStruct((SUB, LANES), f32),
            jax.ShapeDtypeStruct((rows, cols), f32),
            jax.ShapeDtypeStruct((rows, cols), f32),
            jax.ShapeDtypeStruct((months, rows, cols), f32),
            jax.ShapeDtypeStruct((months, rows, cols), f32),
        ],
        compiler_params=params_of(16),
        name="pack_edges",
    )(pos, fin, nxt, sea, prey, heat, *fleet_blocks, *[rate.reshape(1, ages) for rate in rates])


def recruit_kernel(c, terms, *refs):
    pos_ref, par_ref, parv_ref, sea_ref, yield_ref, fish_ref, nxt_ref = refs[:7]
    term_refs = refs[7 : 7 + terms]
    rowc, colw, cole, catch, _ = refs[7 + terms : 12 + terms]
    all_ref, ahead_out, back_out, east_out, west_out, both_out, recruit_out, last_out, top, bottom = refs[12 + terms :]
    rows, cols, ages, months = c.rows, c.cols, c.ages, c.months
    n_i, n_j = rows // SUB, cols // LANES
    keep = (pos_ref[0] < c.sizes[0] - 1).astype(f32)
    spawning = functools.reduce(jnp.add, [r[c.month] for r in term_refs])
    first = functools.reduce(jnp.add, [r[months] for r in term_refs])
    ratio = 1.0 / (1.0 + spawning)
    recruit_out[...] = first * sea_ref[...].astype(f32) * yield_ref[...] * ratio * ratio
    last = (nxt_ref[0:rows, :] + recruit_out[...] * nxt_ref[rows : rows + 1, :]) * keep
    last_out[...] = last

    def body(h, carry):
        for k in range(BATCH):
            a = h * BATCH + k
            mat = par_ref[MAT, a]
            for i in range(n_i):
                for j in range(n_j):
                    ys, xs = slice(i * SUB, (i + 1) * SUB), slice(j * LANES, (j + 1) * LANES)
                    value = at_edges(
                        c, i, j, a, all_ref[a, ys, xs], fish_ref, rowc, colw, cole, catch.at[c.month]
                    )
                    value = value + recruit_out[ys, xs] * mat
                    all_ref[a, ys, xs] = value
                    if i == 0:
                        top[j, pl.ds(a, 1), :] = value[0:1]
                    if i == n_i - 1:
                        bottom[j, pl.ds(a, 1), :] = value[SUB - 1 : SUB]
        return carry

    lax.fori_loop(0, ages // BATCH, body, 0)
    place = lax.broadcasted_iota(jnp.int32, (ages, cols), 0)
    for src, dst, row in ((top, back_out, 0), (bottom, ahead_out, rows - 1)):
        full = jnp.concatenate([src[j] for j in range(n_j)], axis=1)
        dst[...] = jnp.where(place == ages - 1, last[row : row + 1, :], pltpu.roll(full, ages - 1, 0))
    lane = lax.broadcasted_iota(jnp.int32, (SUB, LANES), 1)
    for i in range(n_i):
        rs = slice(i * SUB, (i + 1) * SUB)
        for dst, lo, by, col in ((west_out, 0, 0, 0), (east_out, cols - LANES, 1, cols - 1)):
            found = jnp.where(lane == ages - 1, last_out[rs, col : col + 1], 0.0)
            for k in range(1, ages):
                value = all_ref[k, rs, lo : lo + LANES]
                found = jnp.where(lane == k - 1, pltpu.roll(value, k - 1 + by, 1) if k - 1 + by else value, found)
            dst[rs, :] = found
    both_out[...] = jnp.where(pos_ref[2] == 0, east_out[...], west_out[...])


def recruit_edges(sizes, pos, par, sea, yields, fish, nxt, terms, edges, catch, inner):
    ages, rows, cols = inner.shape
    months = terms[0].shape[0] - 1
    c = Cfg(rows=rows, cols=cols, ages=ages, months=months, month=months - 1, sizes=sizes)
    line = jax.ShapeDtypeStruct((ages, cols), f32)
    column = jax.ShapeDtypeStruct((rows, LANES), f32)
    operands = [pos, par, par, sea, yields, fish, nxt, *terms, *edges, catch, inner]
    return pl.pallas_call(
        functools.partial(recruit_kernel, c, len(terms)),
        in_specs=[whole(SMEM), whole(SMEM)] + [whole()] * (len(operands) - 2),
        out_specs=[whole()] * 8,
        out_shape=[jax.ShapeDtypeStruct(inner.shape, f32), line, line, column, column, column]
        + [jax.ShapeDtypeStruct((rows, cols), f32)] * 2,
        scratch_shapes=[pltpu.VMEM((cols // LANES, ages, LANES), f32)] * 2,
        input_output_aliases={len(operands) - 1: 0},
        cost_estimate=pl.CostEstimate(flops=16 * inner.size, bytes_accessed=8 * inner.size, transcendentals=0),
        compiler_params=params_of(8),
        name="recruit_edges",
    )(*operands)


class Cfg:
    def __init__(self, **kw):
        self.__dict__.update(kw)


def column_of(par_ref, k, ages):
    down = lax.broadcasted_iota(jnp.int32, (ages, LANES), 0)
    across = lax.broadcasted_iota(jnp.int32, (ages, LANES), 1)
    row = jnp.broadcast_to(par_ref[k : k + 1, :], (ages, LANES))
    return jnp.sum(jnp.where(down == across, row, 0.0), axis=1, keepdims=True)


def edge_flux(c, pos_ref, parv_ref, sea_ref, forage_ref, heat4_ref, own, got, msgs, rowc, colw, cole, fish_ref=None):
    rows, cols, ages = c.rows, c.cols, c.ages
    n_coh, n_lat, n_lon = c.sizes
    own_ahead, own_back, own_east, own_west = own
    from_before, from_after, from_west, from_east = got
    msg_before, msg_after, msg_west, msg_east = msgs
    sea_line, prey_line, heat_line = ages, ages + 1 + 2 * c.month, ages + 2 + 2 * c.month
    kappa, tau, ideal, death, gear2 = (column_of(parv_ref, k, ages) for k in (KAPPA, TAU, IDEAL, DEATH, GEAR2))
    has = [
        (pos_ref[1] > 0).astype(f32),
        (pos_ref[1] < n_lat - 1).astype(f32),
        (pos_ref[2] > 0).astype(f32),
        (pos_ref[2] < n_lon - 1).astype(f32),
    ]
    for k, (row, own, got, msg) in enumerate(
        ((0, own_back, from_before, msg_before), (rows - 1, own_ahead, from_after, msg_after))
    ):
        here = habitat_of(forage_ref[row : row + 1, :], heat4_ref[row : row + 1, :], ideal, tau)
        sea_there = msg[sea_line : sea_line + 1, :]
        there = habitat_of(
            sea_there * msg[prey_line : prey_line + 1, :], msg[heat_line : heat_line + 1, :] * 0.25, ideal, tau
        )
        both = sea_ref[row : row + 1, :].astype(f32) * sea_there * has[k]
        flux = both * (kappa + jnp.maximum(there - here, 0.0)) * (own[0:ages, :] - got[0:ages, :])
        if fish_ref is not None:
            flux = flux * jnp.exp2(death - gear2 * fish_ref[row : row + 1, :])
        for j in range(cols // LANES):
            rowc[k, j] = flux[:, j * LANES : (j + 1) * LANES]
    kappa, tau, ideal, death, gear2 = (parv_ref[k : k + 1, :] for k in (KAPPA, TAU, IDEAL, DEATH, GEAR2))
    for k, (col, own, got, msg, dst) in enumerate(
        ((0, own_west, from_west, msg_west, colw), (cols - 1, own_east, from_east, msg_east, cole))
    ):
        here = habitat_of(forage_ref[:, col : col + 1], heat4_ref[:, col : col + 1], ideal, tau)
        msg = msg.at[0:rows]
        sea_there = msg[:, sea_line : sea_line + 1]
        there = habitat_of(
            sea_there * msg[:, prey_line : prey_line + 1], msg[:, heat_line : heat_line + 1] * 0.25, ideal, tau
        )
        both = sea_ref[:, col : col + 1].astype(f32) * sea_there * has[2 + k]
        flux = both * (kappa + jnp.maximum(there - here, 0.0)) * (own[0:rows, :] - got[0:rows, :])
        if fish_ref is not None:
            flux = flux * jnp.exp2(death - gear2 * fish_ref[:, col : col + 1])
        dst[...] = flux


def advance(c, k, a, par_ref, load, tables, out_ref, recruit=None):
    openv, openh, forage, heat4, fish_ref, *edges = tables
    if edges:
        rowc, colw, cole, catch = edges
    n_i, n_j = c.rows // SUB, c.cols // LANES
    lane = lax.broadcasted_iota(jnp.int32, (SUB, LANES), 1)
    sub = lax.broadcasted_iota(jnp.int32, (SUB, LANES), 0)
    kappa, tau, ideal = par_ref[KAPPA, a], par_ref[TAU, a], par_ref[IDEAL, a]
    death, gear2 = par_ref[DEATH, a], par_ref[GEAR2, a]
    if recruit is not None:
        mat = par_ref[MAT, a]

    def tile(i, j):
        return slice(i * SUB, (i + 1) * SUB), slice(j * LANES, (j + 1) * LANES)

    def strip(i):
        adj, hab = [], []
        for j in range(n_j):
            at = tile(i, j)
            adj.append(load(*at))
            off = heat4[at] - ideal
            hab.append(forage[at] * tau * pl.reciprocal(1.0 + off * off, approx=False))
        return adj, hab, [pltpu.roll(v, SUB - 1, 0) for v in adj], [pltpu.roll(v, SUB - 1, 0) for v in hab]

    now = strip(0)
    above = [jnp.zeros((SUB, LANES), f32)] * n_j
    if edges:
        above = [jnp.broadcast_to(-rowc[0, j, pl.ds(a, 1), :], (SUB, LANES)) for j in range(n_j)]
        below = [jnp.broadcast_to(rowc[1, j, pl.ds(a, 1), :], (SUB, LANES)) for j in range(n_j)]
    for i in range(n_i):
        after = strip(i + 1) if i + 1 < n_i else now
        adj, hab, adj_up, hab_up = now
        out = [None] * n_j
        for j in range(n_j):
            at = tile(i, j)
            adj_d = jnp.where(sub == SUB - 1, after[2][j], adj_up[j])
            hab_d = jnp.where(sub == SUB - 1, after[3][j], hab_up[j])
            g = hab_d - hab[j]
            d = openv[at] * (adj[j] - adj_d)
            p = jnp.maximum(g, 0.0) + kappa
            f = p * d
            if edges and i == n_i - 1:
                f = jnp.where(sub == SUB - 1, below[j], f)
            turned = pltpu.roll((p - g) * d, 1, 0)
            out[j] = f - jnp.where(sub == 0, above[j], turned)
            above[j] = turned
        adj_l = [pltpu.roll(v, LANES - 1, 1) for v in adj]
        hab_l = [pltpu.roll(v, LANES - 1, 1) for v in hab]
        flows, backs = [], []
        for j in range(n_j):
            at = tile(i, j)
            if j + 1 < n_j:
                adj_d = jnp.where(lane == LANES - 1, adj_l[j + 1], adj_l[j])
                hab_d = jnp.where(lane == LANES - 1, hab_l[j + 1], hab_l[j])
            else:
                adj_d, hab_d = adj_l[j], hab_l[j]
            g = hab_d - hab[j]
            d = openh[at] * (adj[j] - adj_d)
            p = jnp.maximum(g, 0.0) + kappa
            flows.append(p * d)
            backs.append(pltpu.roll((p - g) * d, 1, 1))
        rs = slice(i * SUB, (i + 1) * SUB)
        if edges:
            edge_e = pltpu.roll(cole[rs, :], (2 * LANES - 1) - a, 1)
            edge_w = pltpu.roll(-colw[rs, :], LANES - a, 1)
            flows[-1] = jnp.where(lane == LANES - 1, edge_e, flows[-1])
        else:
            edge_w = jnp.zeros((SUB, LANES), f32)
        for j in range(n_j):
            at = tile(i, j)
            came = jnp.where(lane == 0, backs[j - 1] if j else edge_w, backs[j])
            moved = adj[j] - (out[j] + flows[j] - came)
            fish = fish_ref[at]
            survive = jnp.exp2(death - gear2 * fish)
            value = survive * moved
            if edges:
                value = value + fish * catch[i * SUB // BY, j, pl.ds(a, 1), :]
            if recruit is not None:
                value = value + recruit[at] * mat
            out_ref[(k,) + at] = value
        now = after


def at_edges(c, i, j, a, value, fish_ref, rowc, colw, cole, catch):
    lane = lax.broadcasted_iota(jnp.int32, (SUB, LANES), 1)
    sub = lax.broadcasted_iota(jnp.int32, (SUB, LANES), 0)
    rs = slice(i * SUB, (i + 1) * SUB)
    n_i, n_j = c.rows // SUB, c.cols // LANES
    value = value + fish_ref[rs, j * LANES : (j + 1) * LANES] * catch[i * SUB // BY, j, pl.ds(a, 1), :]
    if i == 0:
        value = value - jnp.where(sub == 0, rowc[0, j, pl.ds(a, 1), :], 0.0)
    if i == n_i - 1:
        value = value - jnp.where(sub == SUB - 1, rowc[1, j, pl.ds(a, 1), :], 0.0)
    if j == 0:
        value = value - jnp.where(lane == 0, pltpu.roll(colw[rs, :], LANES - a, 1), 0.0)
    if j == n_j - 1:
        value = value - jnp.where(lane == LANES - 1, pltpu.roll(cole[rs, :], (2 * LANES - 1) - a, 1), 0.0)
    return value


def read_plane(ref, k, ys, xs):
    if ref.dtype == f32:
        return ref[k, ys, xs]
    low = ys.start // 16 * 16
    wide = ref[k, low : low + 16, xs].astype(f32)
    return wide[ys.start - low : ys.stop - low]


def all_cohorts(c, step, count, par_ref, later_ref, next_ref, recruit_ref, go):
    def loader(a):
        def load(ys, xs):
            value = read_plane(later_ref, a + 1, ys, xs)
            if recruit_ref is not None:
                value = value + recruit_ref[ys, xs] * par_ref[MAT, a + 1]
            return value

        return load

    def body(h, carry):
        for k in range(PAIR):
            go(h * PAIR + k, step * count + h * PAIR + k, loader(step * count + h * PAIR + k))
        return carry

    final = step == c.ages // count - 1
    turns = count // PAIR
    fixed = isinstance(step, int)
    if fixed:
        lax.fori_loop(0, turns - 1 if final else turns, body, 0)
    else:
        lax.fori_loop(0, jnp.where(final, turns - 1, turns), body, 0)

    def rest():
        for k in range(count - PAIR, count):
            a = c.ages - count + k
            go(k, a, loader(a) if a + 1 < c.ages else lambda ys, xs: next_ref[ys, xs])

    if not fixed:
        pl.when(final)(rest)
    elif final:
        rest()


def first_kernel(c, *refs):
    refs = list(refs)

    def take(n):
        out = refs[:n]
        del refs[:n]
        return out

    pos_ref, parv_ref, inner_ref = take(3)
    own, got = take(4), take(4)
    sea_ref, fish_ref = take(2)
    fleet_refs = take(c.n_fleet)
    forage, heat4 = take(2)
    plane_out, rowc, colw, cole, catch = take(5)
    rows, cols, ages, months = c.rows, c.cols, c.ages, c.months
    blocks_y, blocks_x = rows // BY, cols // BX
    edge_flux(c, pos_ref, parv_ref, sea_ref, forage.at[c.month], heat4.at[c.month], own, got, got, rowc, colw, cole, fish_ref)

    flat = jnp.concatenate([ref[...] for ref in fleet_refs], axis=0)
    names = flat[:, months * ages : months * ages + 1]
    turned = flat.T[0 : months * ages]
    base = ((pos_ref[1] * c.sizes[2] + pos_ref[2]) * (blocks_y * blocks_x)).astype(f32)
    block_col = (lax.broadcasted_iota(jnp.int32, (flat.shape[0], cols), 1) // BX).astype(f32)
    gear = column_of(parv_ref, GEAR, ages)
    for by in range(blocks_y):
        named = (block_col == names - (base + by * blocks_x)).astype(f32)
        sums = jnp.dot(turned, named, precision=lax.Precision.HIGHEST, preferred_element_type=f32)
        for t in range(months):
            for j in range(cols // LANES):
                catch[t, by, j] = gear * sums[t * ages : (t + 1) * ages, j * LANES : (j + 1) * LANES]

    for i in range(rows // SUB):
        for j in range(cols // LANES):
            ys, xs = slice(i * SUB, (i + 1) * SUB), slice(j * LANES, (j + 1) * LANES)
            plane_out[0, ys, xs] = at_edges(
                c, i, j, 0, inner_ref[0, ys, xs], fish_ref, rowc, colw, cole, catch.at[c.month]
            )
    plane_out[0, rows : rows + SUB, :] = jnp.broadcast_to(
        jnp.broadcast_to(parv_ref[MAT : MAT + 1, 0:1], (1, cols)), (SUB, cols)
    )


def month_kernel(c, *refs):
    par_ref, later_ref, next_ref, fish_ref, openv, openh, forage, heat4 = refs[:8]
    out_ref = refs[-1]
    tables = (openv, openh, forage.at[c.month], heat4.at[c.month], fish_ref)

    def go(k, a, load):
        advance(c, a, a, par_ref, load, tables, out_ref)

    all_cohorts(c, c.part, c.ages // PARTS, par_ref, later_ref, next_ref, None, go)


def last_kernel(c, *refs):
    refs = list(refs)

    def take(n):
        out = refs[:n]
        del refs[:n]
        return out

    pos_ref, par_ref, parv_ref, later_ref, next_ref, recruit_ref, sea_ref, fish_ref, yield_ref = take(9)
    openv, openh, forage, heat4, catch = take(5)
    own, got, msgs = take(4), take(4), take(4)
    term_refs = take(c.n_terms)
    bcast_refs = take(c.n_bcast)
    out_ref, grad_ref = take(2)
    rowc, colw, cole, final_recruit = take(4)
    rows, months = c.rows, c.months
    step = pl.program_id(0)

    @pl.when(step == 0)
    def _():
        edge_flux(
            c, pos_ref, parv_ref, sea_ref, forage.at[c.month], heat4.at[c.month], own, got, msgs, rowc, colw, cole
        )
        sea = sea_ref[...].astype(f32)
        totals = [functools.reduce(jnp.add, [r[t] for r in term_refs]) for t in range(months + 1)]
        first = bcast_refs[0][...] * (pos_ref[0] == 0).astype(f32)
        first = first + bcast_refs[1][...] * (pos_ref[0] == c.sizes[0] - 1).astype(f32)
        for ref in bcast_refs[2:]:
            first = first + ref[...]
        first = first[0:rows] + recruit_ref[...] * first[rows : rows + 1]
        ratios = [1.0 / (1.0 + totals[t]) for t in range(months)]
        grad_ref[...] = (totals[months] * totals[1] * ratios[1] + first * totals[0] * ratios[0]) * sea
        final_recruit[...] = first * sea * yield_ref[...] * ratios[0] * ratios[0]

    tables = (openv, openh, forage.at[c.month], heat4.at[c.month], fish_ref, rowc, colw, cole, catch.at[c.month])

    def go(k, a, load):
        advance(c, k, a, par_ref, load, tables, out_ref, recruit=final_recruit)

    all_cohorts(c, step, GROUP, par_ref, later_ref, next_ref, None, go)


def cost(planes, rows, cols):
    cells = planes * rows * cols
    return pl.CostEstimate(flops=60 * cells, bytes_accessed=8 * cells, transcendentals=2 * cells)


def edge_shapes(ages, rows, cols):
    return [
        jax.ShapeDtypeStruct((2, cols // LANES, ages, LANES), f32),
        jax.ShapeDtypeStruct((rows, LANES), f32),
        jax.ShapeDtypeStruct((rows, LANES), f32),
    ]


def first_cohort(sizes, pos, par, inner, own, got, sea, fish, fleet_blocks, forage, heat4):
    ages, rows, cols = inner.shape
    months = forage.shape[0]
    c = Cfg(rows=rows, cols=cols, ages=ages, months=months, month=months - 1, sizes=sizes, n_fleet=len(fleet_blocks))
    operands = [pos, par, inner, *own, *got, sea, fish]
    at = len(operands)
    operands += [block for block, _ in fleet_blocks] + [forage, heat4]

    def kernel(*refs):
        refs = list(refs)
        for k, (block, start) in enumerate(fleet_blocks):
            if start:
                refs[at + k] = refs[at + k].at[start : block.shape[0]]
        first_kernel(c, *refs)

    out_shape = [jax.ShapeDtypeStruct((1, rows + SUB, cols), f32)]
    out_shape += edge_shapes(ages, rows, cols)
    out_shape.append(jax.ShapeDtypeStruct((months, rows // BY, cols // LANES, ages, LANES), f32))
    return pl.pallas_call(
        kernel,
        in_specs=[whole(SMEM)] + [whole()] * (len(operands) - 1),
        out_specs=[whole()] * len(out_shape),
        out_shape=out_shape,
        cost_estimate=cost(4, rows, cols),
        compiler_params=params_of(8),
        name="first_cohort",
    )(*operands)


def month_inner(sizes, part, par, fin, nxt, fish, fields, before, ahead_of):
    ages, rows, cols = fin.shape
    months = fields[2].shape[0]
    c = Cfg(rows=rows, cols=cols, ages=ages, months=months, month=months - 1, sizes=sizes, part=part)
    operands = [par, fin, nxt, fish, *fields, ahead_of]
    specs = [whole(SMEM)] + [whole()] * (len(operands) - 2) + [pl.BlockSpec(memory_space=pl.ANY)]
    alias = {}
    if before is not None:
        alias = {len(operands): 0}
        operands.append(before)
        specs.append(whole())
    return pl.pallas_call(
        functools.partial(month_kernel, c),
        in_specs=specs,
        out_specs=whole(),
        out_shape=jax.ShapeDtypeStruct((ages, rows, cols), f32),
        input_output_aliases=alias,
        cost_estimate=cost(ages // PARTS, rows, cols),
        compiler_params=params_of(16),
        name="month_inner",
    )(*operands)


def month_last(sizes, pos, par, later, nxt, recruit, sea, fish, yields, fields, catch, own, got, msgs, terms, bcasts):
    ages, rows, cols = later.shape
    months = catch.shape[0]
    c = Cfg(
        rows=rows, cols=cols, ages=ages, months=months, month=0, sizes=sizes, n_terms=len(terms), n_bcast=len(bcasts)
    )
    operands = [pos, par, par, later, nxt, recruit, sea, fish, yields, *fields, catch, *own, *got, *msgs]
    operands += [*terms, *bcasts]
    scratch = [pltpu.VMEM(x.shape, f32) for x in edge_shapes(ages, rows, cols)]
    return pl.pallas_call(
        functools.partial(last_kernel, c),
        grid=(ages // GROUP,),
        in_specs=[whole(SMEM), whole(SMEM)] + [whole()] * (len(operands) - 2),
        out_specs=[pl.BlockSpec((GROUP, rows, cols), lambda i: (i, 0, 0)), whole()],
        out_shape=[jax.ShapeDtypeStruct((ages, rows, cols), f32), jax.ShapeDtypeStruct((rows, cols), f32)],
        scratch_shapes=scratch + [pltpu.VMEM((rows, cols), f32)],
        cost_estimate=cost(ages, rows, cols),
        compiler_params=params_of(16),
        name="month_last",
    )(*operands)


def habitat_of(forage, heat, ideal, tau):
    off = heat - ideal
    return forage * (tau / (1.0 + off * off))


def shards(
    saved,
    fin,
    prey,
    heat,
    sea,
    fish,
    yields,
    death,
    gear,
    kappa,
    tau,
    ideal,
    breeding,
    landing,
    east_piece,
    north_piece,
    patch,
    bounds,
):
    months, ages, rows, cols = saved.shape
    n_coh, n_lat, n_lon = sizes = tuple(lax.axis_size(axis) for axis in ("coh", "lat", "lon"))
    at_coh, at_lat, at_lon = (lax.axis_index(axis) for axis in ("coh", "lat", "lon"))
    pos = jnp.stack([at_coh, at_lat, at_lon]).astype(jnp.int32)
    cohort_age = at_coh * ages + jnp.arange(ages)
    nblocks = (rows // BY) * (cols // BX)
    inside = (cohort_age[None, :] >= bounds[:, 0:1]) & (cohort_age[None, :] < bounds[:, 1:2])
    masked = (landing * inside[:, None, :].astype(f32)).reshape(landing.shape[0], months * ages)
    names = ((north_piece * n_lon + east_piece[:, 0]) * nblocks + patch).astype(f32)
    fleet = jnp.concatenate([masked, names[:, None]], axis=1)
    fleet = jnp.pad(fleet, ((0, 0), (0, LANES - fleet.shape[1])))

    first = fin[0].astype(f32)
    nxt = shift(first, "coh", -1)
    terms = first_terms(spawn_parts(pos, breeding, ages * n_coh, saved, first, first), "coh")

    ahead, back, east, west, fleet_pack, later_last, par, *fields = pack_edges(
        sizes, pos, fin, nxt, sea, prey, heat, [fleet], (death, gear, kappa, tau, ideal, breeding)
    )
    from_before, from_after = shift(ahead, "lat", 1), shift(back, "lat", -1)
    blocks = [ahead, from_before] + ([from_after] if n_lat > 2 else [])
    blocks += [shift(fleet_pack, "lat", d) for d in range(2, n_lat - 1)]
    inner = month_inner(sizes, 0, par, fin, later_last, fish, fields, None, ahead)
    both, gathered = relay(pos, east, west, inner, blocks, fleet_pack.shape[0])
    terms = other_terms(terms, "coh", both)
    inner = month_inner(sizes, 1, par, fin, later_last, fish, fields, inner, both)
    from_west, from_east = swap_edges(east, west, both, "lon")
    fleet_blocks = [(gathered, 0)]
    if n_lon == 2:
        fleet_blocks.append((from_west, rows))
    else:
        fleet_blocks += [(shift(gathered, "lon", d), 0) for d in range(1, n_lon)]
    own = (ahead, back, east, west)
    msgs = (from_before, from_after, from_west, from_east)
    plane, *edges, catch = first_cohort(
        sizes, pos, par, inner, own, msgs, sea, fish, fleet_blocks, fields[2], fields[3]
    )
    plane = plane.reshape(rows + SUB, cols)
    down = shift(plane, "coh", -1)
    bcasts = [plane, down] + [lax.ppermute(plane, "coh", [(0, j)]) for j in range(1, n_coh - 1)]
    later, ahead, back, east, west, both, recruit, nxt = recruit_edges(
        sizes, pos, par, sea, yields, fish, down, terms, edges, catch, inner
    )
    own = (ahead, back, east, west)
    got = (shift(ahead, "lat", 1), shift(back, "lat", -1), *swap_edges(east, west, both, "lon"))
    return tuple(
        month_last(
            sizes, pos, par, later, nxt, recruit, sea, fish, yields, fields, catch, own, got, msgs, terms, bcasts
        )
    )


def solution(mesh):
    in_specs = (
        P(None, "coh", "lat", "lon"),
        P("coh", "lat", "lon"),
        P(None, "lat", "lon"),
        P(None, "lat", "lon"),
        P("lat", "lon"),
        P("lat", "lon"),
        P("lat", "lon"),
        P("coh"),
        P("coh"),
        P("coh"),
        P("coh"),
        P("coh"),
        P("coh"),
        P(("lat", "lon"), None, "coh"),
        P(("lat", "lon"), None),
        P(("lat", "lon")),
        P(("lat", "lon")),
        P(("lat", "lon"), None),
    )
    out_specs = (P("coh", "lat", "lon"), P("lat", "lon"))

    return jax.shard_map(shards, mesh=mesh, in_specs=in_specs, out_specs=out_specs, check_vma=False)
```
